32 devices in a mesh: dp: 8 (over z, y), seq: 4 (over x, core).
Axes of the slice: x: 2, y: 2, z: 4, core: 2. Of those that a mesh axis runs over, the one named last changes fastest.
Arguments:
- tokens: bfloat16 [128, 512, 768], P('dp', 'seq'), may hold values from -6 to 6
- sources: int32 [128], replicated, may hold values from 0 to 1, as said below
- lengths: int32 [128], P('dp'), may hold values from 64 to 512, as said below
- pairing: int32 [128], replicated, may hold values from 0 to 127, each once
- queries: bfloat16 [128, 768], P('dp'), may hold values from -6 to 6
- w_query: bfloat16 [768, 768], replicated, may hold values from -0.375 to 0.375
- b_query: float32 [768], replicated, may hold values from -1.5 to 1.5
- w_key: bfloat16 [768, 768], replicated, may hold values from -0.375 to 0.375
- w_value: bfloat16 [768, 768], replicated, may hold values from -0.21875 to 0.21875
- b_value: float32 [768], replicated, may hold values from -1.5 to 1.5
- w_out: bfloat16 [768, 768], replicated, may hold values from -0.4375 to 0.4375
- b_out: float32 [768], replicated, may hold values from -3 to 3
- gain_one: float32 [768], replicated, may hold values from 0.5 to 1.5
- shift_one: float32 [768], replicated, may hold values from -1 to 1
- w_up: bfloat16 [768, 3072], replicated, may hold values from -0.21875 to 0.21875
- b_up: float32 [3072], replicated, may hold values from -0.6 to 0.6
- w_down: bfloat16 [3072, 768], replicated, may hold values from -0.109375 to 0.109375
- second_feedforward_offset: float32 [768], replicated, may hold values from -3 to 3
- gain_two: float32 [768], replicated, may hold values from 0.5 to 1.5
- shift_two: float32 [768], replicated, may hold values from -1 to 1
Outputs:
- loss: float32 [], replicated
- activations: bfloat16 [128, 512, 768], P('dp', 'seq')
- grad_tokens: float32 [128, 512, 768], P('dp', 'seq')
- grad_w_query: float32 [768, 768], replicated
- grad_b_query: float32 [768], replicated
- grad_w_key: float32 [768, 768], replicated
- grad_w_value: float32 [768, 768], replicated
- grad_b_value: float32 [768], replicated
- grad_w_out: float32 [768, 768], replicated
- grad_b_out: float32 [768], replicated
- grad_gain_one: float32 [768], replicated
- grad_shift_one: float32 [768], replicated
- grad_w_up: float32 [768, 3072], replicated
- grad_b_up: float32 [3072], replicated
- grad_w_down: float32 [3072, 768], replicated
- grad_b_down: float32 [768], replicated
- grad_gain_two: float32 [768], replicated
- grad_shift_two: float32 [768], replicated
The draws below stay inside these ranges and needn't reach their ends.
Inputs may be any that keep to these rules, and one draw needn't show every extreme that they name: Source 0 passages have lengths 512 // 8 to 256, source 1 passages 512 // 2 to 512; passage 0 has length 64 and passage 128 - 1 length 512. `sources`: passage 0 is of source 0 and passage 128 - 1 of source 1. `pairing`: each passage is the positive of exactly one query.
All inputs are finite; a program needn't handle non-finite values.
Results may differ from the reference program's by a relative error of at most 0.014.
The reference program's roundings to bfloat16 on the way count: a program that leaves them out, or rounds other values in their place, can miss the bound.
Values may be sent and summed in bfloat16 or wider, within the bound.
No kernel may reach another device: no remote copies, remote signals or barrier semaphores. Data moves between devices by JAX's collectives and lax.ppermute only.
A program may use at most 448 MiB of HBM per device.

```python
import math
import jax
import jax.numpy as jnp
from jax import lax

D = 768
HEADS = 12
FF = 3072
L = 512
B = 128


def source_and_length(key):
    base = jax.random.fold_in(key, 17)
    key_one, key_two, key_three = jax.random.split(base, 3)
    position = jnp.arange(B, dtype=jnp.int32)
    anchor = jax.random.randint(key_one, (B,), 0, 2)
    anchor = jnp.where(position == 0, 0, jnp.where(position == B - 1, 1, anchor))
    short_len = jax.random.randint(key_two, (B,), L // 8, L // 2 + 1)
    long_len = jax.random.randint(key_three, (B,), L // 2, L + 1)
    lens = jnp.where(anchor == 0, short_len, long_len)
    lens = jnp.where(position == 0, L // 8, jnp.where(position == B - 1, L, lens))
    return (anchor.astype(jnp.int32), lens.astype(jnp.int32))


def draw_sources(key, part):
    return source_and_length(key)[0]


def draw_lengths(key, part):
    return source_and_length(key)[1]


def steps_of(key, shape, shards, least, top_value):
    factor_of = 1.0
    for axis_at, parts in shards:
        steps = jax.random.uniform(jax.random.fold_in(jax.random.fold_in(key, 6), axis_at), (parts,), jnp.float32, least / len(shards), top_value / len(shards))
        factor_of = factor_of * jnp.repeat(jnp.exp(steps), shape[axis_at] // parts).reshape((-1,) + (1,) * (len(shape) - 1 - axis_at))
    return factor_of


def gaussian(key, dims, scale, limit, pieces=(), held_as=jnp.bfloat16):
    level = steps_of(key, dims, pieces, -0.22, 0.18) if pieces else 1.0
    entries = jax.random.normal(key, dims, jnp.float32) * scale * level
    return jnp.minimum(jnp.maximum(entries, -limit), limit).astype(held_as)


def setup_inputs(seed: int = 0) -> dict:
    keys = jax.random.split(jax.random.key(seed), 21)
    return {
        "tokens": gaussian(keys[0], (B, L, D), 1.0, 6.0, ((0, 8), (1, 4))),
        "sources": draw_sources(jax.random.fold_in(keys[20], 71), 0),
        "lengths": draw_lengths(jax.random.fold_in(keys[20], 71), 0),
        "pairing": jax.random.permutation(keys[3], B).astype(jnp.int32),
        "queries": gaussian(keys[4], (B, D), 1.0, 6.0, ((0, 8),)),
        "w_query": gaussian(keys[5], (D, D), (D // 3) ** -0.5, 0.375),
        "b_query": gaussian(keys[6], (D,), 0.25, 1.5, (), jnp.float32),
        "w_key": gaussian(keys[7], (D, D), (D // 3) ** -0.5, 0.375),
        "w_value": gaussian(keys[8], (D, D), D ** -0.5, 0.21875),
        "b_value": gaussian(keys[9], (D,), 0.25, 1.5, (), jnp.float32),
        "w_out": gaussian(keys[10], (D, D), (D // 4) ** -0.5, 0.4375),
        "b_out": gaussian(keys[11], (D,), 0.5, 3.0, (), jnp.float32),
        "gain_one": jnp.clip(1.0 + 0.1 * jax.random.normal(keys[12], (D,), jnp.float32), 0.5, 1.5),
        "shift_one": gaussian(keys[13], (D,), 0.1, 1.0, (), jnp.float32),
        "w_up": gaussian(keys[14], (D, FF), D ** -0.5, 0.21875),
        "b_up": gaussian(keys[15], (FF,), 0.1, 0.6, (), jnp.float32),
        "w_down": gaussian(keys[16], (FF, D), FF ** -0.5, 0.109375),
        "second_feedforward_offset": gaussian(keys[17], (D,), 0.5, 3.0, (), jnp.float32),
        "gain_two": jnp.clip(1.0 + 0.1 * jax.random.normal(keys[18], (D,), jnp.float32), 0.5, 1.5),
        "shift_two": gaussian(keys[19], (D,), 0.1, 1.0, (), jnp.float32),
    }


largest_cosine_score = lax.Precision.HIGHEST
epsilon = 1e-05
contrast_sharpness_divisor = 0.01

@jax.custom_vjp
def low(v):
    return lax.optimization_barrier(v.astype(jnp.bfloat16)).astype(jnp.float32)

@jax.custom_vjp
def low_back(v):
    return v

def low_keep(v):
    return (low(v), None)

def low_pass(kept, grad):
    return (grad,)

def back_keep(v):
    return (v, None)

def back_low(kept, grad):
    return (low(grad),)
low.defvjp(low_keep, low_pass)
low_back.defvjp(back_keep, back_low)

def layer_norm(value, gain, shift):
    centred = value - lax.optimization_barrier(jnp.mean(value, axis=-1, keepdims=True))
    inverse = lax.rsqrt(lax.optimization_barrier(jnp.mean(centred * centred, axis=-1, keepdims=True)) + epsilon)
    return centred * inverse * gain + shift

def matmul(left, weight):
    return jnp.einsum('gtd,de->gte', left, weight, precision=largest_cosine_score)

def layer(params, inputs, lens):
    w_query, b_query, w_key, w_value, b_value, w_out, b_out, gain_one, shift_one, w_up, b_up, w_down, second_feedforward_offset, gain_two, shift_two = params
    group, span, width = inputs.shape
    head_size = width // HEADS
    place = jnp.arange(span, dtype=jnp.int32)[None, :]
    live_keys = place < lens[:, None]
    query = low(low_back(matmul(inputs, w_query) + b_query))
    keyed = low(low_back(matmul(inputs, w_key)))
    valued = low(low_back(matmul(inputs, w_value) + b_value))
    query_h = query.reshape(group, span, HEADS, head_size)
    key_h = keyed.reshape(group, span, HEADS, head_size)
    value_h = valued.reshape(group, span, HEADS, head_size)
    scores = jnp.einsum('gqhd,gkhd->ghqk', query_h, key_h, precision=largest_cosine_score) * head_size ** (-0.5)
    scores = low_back(jnp.where(live_keys[:, None, None, :], scores, -1000000000.0))
    top = lax.optimization_barrier(jnp.max(scores, axis=-1, keepdims=True))
    expo = jnp.exp(scores - top)
    probs = expo / lax.optimization_barrier(jnp.sum(expo, axis=-1, keepdims=True))
    mixed = jnp.einsum('ghqk,gkhd->gqhd', low(probs), value_h, precision=largest_cosine_score)
    mixed = low(low_back(mixed.reshape(group, span, width)))
    branch = low_back(matmul(mixed, w_out) + b_out)
    hidden = layer_norm(inputs + branch, gain_one, shift_one)
    upward = low_back(matmul(low(hidden), w_up) + b_up)
    gelu_low = low(jax.nn.gelu(upward, approximate=False))
    downward = low_back(matmul(gelu_low, w_down) + second_feedforward_offset)
    output = layer_norm(hidden + downward, gain_two, shift_two)
    live_rows = (place < lens[:, None]).astype(jnp.float32)
    pooled = lax.optimization_barrier(jnp.sum(live_rows[:, :, None] * output, axis=1)) / lens.astype(jnp.float32)[:, None]
    return (output, pooled)

def contrast(pooled_all, query_rows, targets, sources):
    document_unit_embedding = pooled_all * lax.rsqrt(lax.optimization_barrier(jnp.sum(pooled_all * pooled_all, axis=-1, keepdims=True)) + 1e-06)
    question_unit_embedding = query_rows * lax.rsqrt(lax.optimization_barrier(jnp.sum(query_rows * query_rows, axis=-1, keepdims=True)) + 1e-06)
    cosine_score_matrix = jnp.dot(question_unit_embedding, document_unit_embedding.T, precision=largest_cosine_score) / contrast_sharpness_divisor
    match = targets[:, None] == jnp.arange(pooled_all.shape[0], dtype=jnp.int32)[None, :]
    query_source = lax.optimization_barrier(jnp.sum(jnp.where(match, sources[None, :], 0), axis=1))
    cosine_score_matrix = jnp.where(query_source[:, None] == sources[None, :], cosine_score_matrix, -1000000000.0)
    top = lax.optimization_barrier(jnp.max(cosine_score_matrix, axis=1, keepdims=True))
    spread = top[:, 0] + jnp.log(lax.optimization_barrier(jnp.sum(jnp.exp(cosine_score_matrix - top), axis=1)))
    chosen = lax.optimization_barrier(jnp.sum(jnp.where(match, cosine_score_matrix, 0.0), axis=1))
    return jnp.sum(spread - chosen)

def reference(tokens, sources, lengths, pairing, queries, w_query, b_query, w_key, w_value, b_value, w_out, b_out, gain_one, shift_one, w_up, b_up, w_down, second_feedforward_offset, gain_two, shift_two):
    params = tuple((item.astype(jnp.float32) for item in (w_query, b_query, w_key, w_value, b_value, w_out, b_out, gain_one, shift_one, w_up, b_up, w_down, second_feedforward_offset, gain_two, shift_two)))
    group = math.gcd(B, max(1, 4096 // L))
    steps = B // group
    inputs = tokens.astype(jnp.float32).reshape(steps, group, L, D)
    lens = lengths.astype(jnp.int32).reshape(steps, group)

    def forward_step(carry, item):
        output, pooled = layer(params, item[0], item[1])
        return (carry, (output.astype(jnp.bfloat16), pooled))
    _, (layer_outputs, pooled_groups) = lax.scan(forward_step, jnp.int32(0), (inputs, lens))
    pooled_flat = pooled_groups.reshape(B, D)
    query_rows = queries.astype(jnp.float32)
    loss, loss_back = jax.vjp(lambda whole: contrast(whole, query_rows, pairing, sources) / B, pooled_flat)
    grad_pooled, = loss_back(jnp.ones_like(loss))
    grad_groups = grad_pooled.reshape(steps, group, D)

    def backward_step(total, item):
        block_in, block_len, block_grad = item
        _, back = jax.vjp(lambda prm, inp: layer(prm, inp, block_len)[1], params, block_in)
        grad_params, grad_inputs = back(block_grad)
        return (jax.tree.map(jnp.add, total, grad_params), grad_inputs)
    zeros = tuple((jnp.zeros_like(item) for item in params))
    totals, grad_inputs = lax.scan(backward_step, zeros, (inputs, lens, grad_groups))
    return (loss, layer_outputs.reshape(B, L, D), grad_inputs.reshape(B, L, D), totals[0], totals[1], totals[2], totals[3], totals[4], totals[5], totals[6], totals[7], totals[8], totals[9], totals[10], totals[11], totals[12], totals[13], totals[14])
```

```python
import jax
import jax.numpy as jnp
from jax import lax
from jax.experimental import pallas as pl
from jax.experimental.pallas import tpu as pltpu
from jax.sharding import PartitionSpec as P

HEADS = 12
EPS = 1e-05
TEMPERATURE = 0.01
MASKED = -1000000000.0
BOTH = ("dp", "seq")
EXACT = lax.Precision.HIGHEST
BF = jnp.bfloat16
F32 = jnp.float32
VMEM_BYTES = 60 * 2**20
BRIEF = pl.CostEstimate(flops=7 * 10**10, bytes_accessed=10**6, transcendentals=0)
TICK = pl.CostEstimate(flops=1000, bytes_accessed=1000, transcendentals=0)


def dot(left, right, left_at=1, right_at=0):
    return lax.dot_general(
        left, right, (((left_at,), (right_at,)), ((), ())), preferred_element_type=F32
    )


def normalize(value):
    centred = value - jnp.mean(value, axis=-1, keepdims=True)
    inverse = lax.rsqrt(jnp.mean(centred * centred, axis=-1, keepdims=True) + EPS)
    return centred * inverse, inverse


def norm_back(grad_unit, unit, inverse):
    first = jnp.mean(grad_unit, axis=-1, keepdims=True)
    second = jnp.mean(grad_unit * unit, axis=-1, keepdims=True)
    return inverse * (grad_unit - first - unit * second)


def gelu_and_slope(value):
    size = jnp.abs(value)
    t = 1.0 / (1.0 + (0.3275911 * 0.7071067811865476) * size)
    bell = jnp.exp(-0.5 * (value * value))
    tail = (
        (((0.5 * 1.061405429 * t - 0.5 * 1.453152027) * t + 0.5 * 1.421413741) * t
         - 0.5 * 0.284496736) * t + 0.5 * 0.254829592
    ) * t * bell
    below = jnp.where(value >= 0.0, 1.0 - tail, tail)
    return value * below, below + value * (bell * 0.3989422804014327)


def lane_half(width, which):
    lanes = lax.broadcasted_iota(jnp.int32, (1, width), 1)
    return ((lanes >= which * (width // 2)) & (lanes < (which + 1) * (width // 2))).astype(F32)


def whole(shape):
    return pl.BlockSpec(shape, lambda i, *_: (0,) * len(shape))


def per_passage(shape, first=0):
    return pl.BlockSpec((1,) + tuple(shape), lambda i, *_: (i + first,) + (0,) * len(shape))


ANYWHERE = pl.BlockSpec(memory_space=pl.ANY)


def fetch(sources, targets, sems):
    return [
        pltpu.make_async_copy(s, t, sems.at[i]) for i, (s, t) in enumerate(zip(sources, targets))
    ]


def forward_kernel(lens, src, *refs, pieces, first, aliased, riders):
    refs = list(refs)
    take = lambda n: [refs.pop(0) for _ in range(n)]
    x_in = take(pieces)
    hbm = take(6)
    (vectors,) = take(1)
    take(aliased + riders)
    (x_all, q_out, k_out, v_out, mixed_out, lse_out, unit_one_out, inverse_one_out,
     hidden_low_out, gelu_out, slope_out, unit_two_out, inverse_two_out, sums_out) = take(14)
    act = take(pieces)
    take(riders)
    held = take(6)
    act_held, sems = take(2)
    w_query, w_key, w_value, w_out, w_up, w_down = held
    b_query, b_value, b_out, gain_one, shift_one, b_down, gain_two, shift_two = (
        vectors[n : n + 1, :] for n in range(8)
    )
    step = pl.program_id(0)
    copies = fetch(hbm, held, sems)

    @pl.when(step == 0)
    def _():
        for copy in copies:
            copy.start()

    def ready(*which):
        @pl.when(step == 0)
        def _():
            for i in which:
                copies[i].wait()

    span, width = x_all.shape[1:]
    block = span // pieces
    head = width // HEADS
    pair = 2 * head
    length = lens[first + step]
    for k in range(pieces):
        x_all[0, pl.ds(pl.multiple_of(src[k] * block, block), block), :] = x_in[k][0]
    x = x_all[0]
    ready(0, 1, 2)
    q_out[0] = ((dot(x, w_query[...]) + b_query) * (head ** -0.5)).astype(BF)
    k_out[0] = dot(x, w_key[...]).astype(BF)
    v_out[0] = (dot(x, w_value[...]) + b_value).astype(BF)
    key_mask = jnp.where(
        lax.broadcasted_iota(jnp.int32, (1, span), 1) < length, 0.0, MASKED
    ).astype(F32)
    lanes = lax.broadcasted_iota(jnp.int32, (1, 128), 1)
    stats = jnp.zeros((span, 128), F32)
    for p in range(HEADS // 2):
        at = slice(p * pair, (p + 1) * pair)
        qp, kp, vp = q_out[0, :, at], k_out[0, :, at], v_out[0, :, at]
        total = None
        for h in range(2):
            half = lane_half(pair, h).astype(BF)
            scores = dot(qp, kp * half, 1, 1) + key_mask
            top = jnp.max(scores, axis=-1, keepdims=True)
            expo = jnp.exp(scores - top)
            norm = jnp.sum(expo, axis=-1, keepdims=True)
            low = (expo * (1.0 / norm)).astype(BF)
            term = dot(low, vp * half)
            total = term if total is None else total + term
            stats = jnp.where(lanes == 2 * p + h, top + jnp.log(norm), stats)
        mixed_out[0, :, at] = total.astype(BF)
    lse_out[0] = stats.T[: lse_out.shape[1]]
    ready(3)
    unit_one, inverse_one = normalize(x.astype(F32) + (dot(mixed_out[0], w_out[...]) + b_out))
    unit_one_out[0] = unit_one
    inverse_one_out[0] = inverse_one
    hidden = unit_one * gain_one + shift_one
    hidden_low = hidden.astype(BF)
    hidden_low_out[0] = hidden_low
    ready(4, 5)
    total = hidden + b_down
    for c in range(gelu_out.shape[2] // width):
        at = slice(c * width, (c + 1) * width)
        value, slope = gelu_and_slope(dot(hidden_low, w_up[:, at]) + vectors[8 + c : 9 + c, :])
        low = value.astype(BF)
        gelu_out[0, :, at] = low
        slope_out[0, :, at] = slope.astype(BF)
        total = total + dot(low, w_down[at, :])
    unit_two, inverse_two = normalize(total)
    unit_two_out[0] = unit_two
    inverse_two_out[0] = inverse_two
    act_held[...] = (unit_two * gain_two + shift_two).astype(BF)
    for k in range(pieces):
        act[k][0] = act_held[pl.ds(pl.multiple_of(src[k] * block, block), block), :]
    live = (lax.broadcasted_iota(jnp.int32, (span, 1), 0) < length).astype(F32)
    sums_out[0] = jnp.sum(unit_two * live, axis=0, keepdims=True)


def forward(lens, src, pieces, weights, vectors, passages, first, before, riders):
    count, block, width = pieces[0].shape
    n = len(pieces)
    span = block * n
    units = weights[4].shape[1]
    shapes = [
        ((span, width), BF), ((span, width), BF), ((span, width), BF), ((span, width), BF),
        ((span, width), BF), ((16, span), F32), ((span, width), F32), ((span, 1), F32),
        ((span, width), BF), ((span, units), BF), ((span, units), BF), ((span, width), F32),
        ((span, 1), F32), ((1, width), F32),
    ]
    outs = [jax.ShapeDtypeStruct((passages,) + s, t) for s, t in shapes]
    outs += [jax.ShapeDtypeStruct((passages, block, width), BF)] * n
    out_specs = [per_passage(o.shape[1:], first) for o in outs]
    kinds = len(outs)
    in_specs = [per_passage((block, width))] * n + [ANYWHERE] * 6 + [whole(vectors.shape)]
    operands = list(pieces) + list(weights) + [vectors]
    aliases = {}
    if before is not None:
        for i, value in enumerate(before):
            aliases[2 + len(operands)] = i
            operands.append(value)
            in_specs.append(ANYWHERE)
    aliases.update(alias(operands, in_specs, outs, out_specs, riders, 2))

    def kernel(*refs):
        forward_kernel(
            *refs, pieces=n, first=first, aliased=0 if before is None else kinds,
            riders=len(riders),
        )

    return pl.pallas_call(
        kernel,
        out_shape=outs,
        grid_spec=pltpu.PrefetchScalarGridSpec(
            num_scalar_prefetch=2,
            grid=(count,),
            in_specs=in_specs,
            out_specs=out_specs,
            scratch_shapes=[pltpu.VMEM(w.shape, BF) for w in weights]
            + [pltpu.VMEM((span, width), BF), pltpu.SemaphoreType.DMA((6,))],
        ),
        input_output_aliases=aliases,
        compiler_params=pltpu.CompilerParams(vmem_limit_bytes=VMEM_BYTES),
        cost_estimate=BRIEF,
    )(lens, src, *operands)


def second_norm_back(length, push, unit_two, inverse_two):
    live = lax.broadcasted_iota(jnp.int32, (unit_two.shape[0], 1), 0) < length
    return jnp.where(live, norm_back(push, unit_two, inverse_two), 0.0)


def hand_over(total, kept_hbm, sent_hbm, side, place, sems):
    half = total.shape[0] // 2
    own = pl.multiple_of(side * half, half)
    other = pl.multiple_of((1 - side) * half, half)
    copies = [
        pltpu.make_async_copy(total.at[pl.ds(at, half), :], out.at[pl.ds(place, half), :], sem)
        for at, out, sem in ((own, kept_hbm, sems.at[0]), (other, sent_hbm, sems.at[1]))
    ]
    for copy in copies:
        copy.start()
    for copy in copies:
        copy.wait()


def alias(operands, specs, outs, out_specs, values, offset):
    pairs = {}
    for value in values:
        pairs[offset + len(operands)] = len(outs)
        operands.append(value)
        specs.append(ANYWHERE)
        outs.append(jax.ShapeDtypeStruct(value.shape, value.dtype))
        out_specs.append(ANYWHERE)
    return pairs


def feed_kernel(lens, core, *refs, part, parts, place, filling, riders):
    refs = list(refs)
    take = lambda n: [refs.pop(0) for _ in range(n)]
    opening, closing = part == 0, part == parts - 1
    if opening:
        push, unit_two, inverse_two = take(3)
    else:
        grad_low_in, grad_hidden_in = take(2)
    if closing:
        unit_one, inverse_one, mixed, gain_one = take(4)
    gelu, slope, hidden_low, w_down, w_up = take(5)
    if closing:
        (w_out,) = take(1)
    take((2 if filling else 0) + riders)
    grad_hidden_out, low_out, up_bias, rows = take(4)
    kept_hbm, sent_hbm = take(2)
    take(riders)
    total, sems = take(2)
    step = pl.program_id(0)
    last = pl.num_programs(0) - 1
    units, width = w_down.shape

    @pl.when(step == 0)
    def _():
        total[...] = jnp.zeros_like(total)
        up_bias[...] = jnp.zeros_like(up_bias)
        rows[...] = jnp.zeros_like(rows)

    if opening:
        grad_hidden = second_norm_back(lens[step], push[0], unit_two[0], inverse_two[0])
        grad_low = grad_hidden.astype(BF)
        low_out[0] = grad_low
        rows[3:4, :] += jnp.sum(grad_low.astype(F32), axis=0, keepdims=True)
    else:
        grad_hidden = grad_hidden_in[0]
        grad_low = grad_low_in[0]
    up_low = (dot(grad_low, w_down[...], 1, 1) * slope[0].astype(F32)).astype(BF)
    total[:units, :] += dot(gelu[0], grad_low, 0, 0)
    up_bias[...] += jnp.sum(up_low.astype(F32), axis=0, keepdims=True)
    total[total.shape[0] - width :, :] += dot(hidden_low[0], up_low, 0, 0)
    grad_hidden = grad_hidden + dot(up_low, w_up[...], 1, 1)
    if closing:
        unit = unit_one[0]
        rows[0:1, :] += jnp.sum(grad_hidden * unit, axis=0, keepdims=True)
        rows[1:2, :] += jnp.sum(grad_hidden, axis=0, keepdims=True)
        grad_one = norm_back(grad_hidden * gain_one[...], unit, inverse_one[0])
        grad_hidden_out[0] = grad_one
        branch_low = grad_one.astype(BF)
        rows[2:3, :] += jnp.sum(branch_low.astype(F32), axis=0, keepdims=True)
        total[units : units + width, :] += dot(mixed[0], branch_low, 0, 0)
        low_out[0] = dot(branch_low, w_out[...], 1, 1).astype(BF)
    else:
        grad_hidden_out[0] = grad_hidden

    @pl.when(step == last)
    def _():
        hand_over(total, kept_hbm, sent_hbm, core[0], place, sems)


def feed_back(lens, core, row_operands, gelu, slope, hidden_low, w_down, w_up, w_out, part, parts,
              place, tall_all, filled, riders):
    opening, closing = part == 0, part == parts - 1
    passages, span, units = gelu.shape
    units //= parts
    width = w_down.shape[1]
    tall = 2 * units + (width if closing else 0)
    tile = per_passage((span, width))
    column = per_passage((span, 1))
    chunk = pl.BlockSpec((1, span, units), lambda i, *_: (i, 0, part))
    specs = [per_passage((1, width)), tile, column] if opening else [tile, tile]
    operands = list(row_operands)
    if closing:
        specs += [tile, column, tile, whole((1, width))]
    operands += [gelu, slope, hidden_low, w_down, w_up]
    specs += [
        chunk, chunk, tile,
        pl.BlockSpec((units, width), lambda i, *_: (part, 0)),
        pl.BlockSpec((width, units), lambda i, *_: (0, part)),
    ]
    if closing:
        operands.append(w_out)
        specs.append(whole((width, width)))
    like = lambda t: jax.ShapeDtypeStruct((passages, span, width), t)
    outs = [
        like(F32), like(BF), jax.ShapeDtypeStruct((1, units), F32),
        jax.ShapeDtypeStruct((8, width), F32),
    ]
    out_specs = [tile, tile, whole((1, units)), whole((8, width))]
    if filled is None:
        outs += [jax.ShapeDtypeStruct((tall_all, width), F32)] * 2
        out_specs += [ANYWHERE] * 2
        pairs = alias(operands, specs, outs, out_specs, riders, 2)
    else:
        pairs = alias(operands, specs, outs, out_specs, tuple(filled) + tuple(riders), 2)

    def kernel(*refs):
        feed_kernel(
            *refs, part=part, parts=parts, place=place, filling=filled is not None,
            riders=len(riders),
        )

    return pl.pallas_call(
        kernel,
        out_shape=outs,
        grid_spec=pltpu.PrefetchScalarGridSpec(
            num_scalar_prefetch=2,
            grid=(passages,),
            in_specs=specs,
            out_specs=out_specs,
            scratch_shapes=[pltpu.VMEM((tall, width), F32), pltpu.SemaphoreType.DMA((2,))],
        ),
        input_output_aliases=pairs,
        compiler_params=pltpu.CompilerParams(vmem_limit_bytes=VMEM_BYTES),
        cost_estimate=BRIEF,
    )(lens, core, *operands)


def attention_kernel(
    lens, src, core, *refs, pieces, final, part, first, opening, closing, filled, riders
):
    refs = list(refs)
    take = lambda n: [refs.pop(0) for _ in range(n)]
    x, q, k, v, lse, grad_mixed, grad_in = take(7)
    weights = take(3)
    if not opening:
        (total_in,) = take(1)
    take(filled + riders)
    out = take(pieces if final else 1)
    (bias,) = take(1)
    totals_out = take(2 if closing else 1)
    take(riders)
    total = take(1)[0]
    lows = take(3)
    tokens_low, sems = take(2)
    step = pl.program_id(0)
    last = pl.num_programs(0) - 1
    span, columns = q.shape[1:]
    width = x.shape[2]
    block = span // pieces
    head = width // HEADS
    pair = 2 * head
    scale = head ** -0.5
    if not opening:
        before = pltpu.make_async_copy(total_in, total, sems.at[0])

    @pl.when(step == 0)
    def _():
        if opening:
            total[...] = jnp.zeros_like(total)
        else:
            before.start()
        bias[...] = jnp.zeros_like(bias)

    key_mask = jnp.where(
        lax.broadcasted_iota(jnp.int32, (span, 1), 0) < lens[first + step], 0.0, MASKED
    ).astype(F32)
    query_low, key_low, value_low = lows
    for p in range(columns // pair):
        at = slice(p * pair, (p + 1) * pair)
        qp, kp, vp, gp = q[0, :, at], k[0, :, at], v[0, :, at], grad_mixed[0, :, at]
        gq = gk = gv = None
        for h in range(2):
            half = lane_half(pair, h).astype(BF)
            qm, gm, km = qp * half, gp * half, kp * half
            n = part * (columns // head) + 2 * p + h
            probs = jnp.exp((dot(kp, qm, 1, 1) + key_mask) - lse[0, n : n + 1, :])
            low = probs.astype(BF)
            grad_probs = dot(vp, gm, 1, 1)
            delta = jnp.sum(probs * grad_probs, axis=0, keepdims=True)
            scores = (probs * (grad_probs - delta)).astype(BF)
            tv = dot(low, gm)
            tk = dot(scores, qm)
            tq = dot(scores, km, 0, 0)
            gv = tv if gv is None else gv + tv
            gk = tk if gk is None else gk + tk
            gq = tq if gq is None else gq + tq
        query_low[:, at] = (gq * scale).astype(BF)
        key_low[:, at] = gk.astype(BF)
        value_low[:, at] = gv.astype(BF)

    if not opening:

        @pl.when(step == 0)
        def _():
            before.wait()

    grad = grad_in[0]
    for n, (low, weight) in enumerate(zip(lows, weights)):
        grad = grad + dot(low[...], weight[...], 1, 1)
        total[:, n * columns : (n + 1) * columns] += dot(x[0], low[...], 0, 0)
    bias[0:1, :] += jnp.sum(query_low[...].astype(F32), axis=0, keepdims=True)
    bias[1:2, :] += jnp.sum(value_low[...].astype(F32), axis=0, keepdims=True)
    if final:
        tokens_low[...] = grad.astype(BF)
        for n in range(pieces):
            out[n][0] = tokens_low[pl.ds(pl.multiple_of(src[n] * block, block), block), :]
    else:
        out[0][0] = grad

    @pl.when(step == last)
    def _():
        if closing:
            hand_over(total, *totals_out, core[0], 0, sems)
        else:
            after = pltpu.make_async_copy(total, totals_out[0], sems.at[1])
            after.start()
            after.wait()


def attention_back(lens, src, core, pieces, x, q, k, v, lse, grad_mixed, grad_in, weights, part,
                   parts, first, count, grad_first, total, closing, before, riders):
    passages, span, width = x.shape
    block = span // pieces
    columns = width // parts
    final = part == parts - 1
    tall = width

    def kernel(*refs):
        attention_kernel(
            *refs, pieces=pieces, final=final, part=part, first=first, opening=total is None,
            closing=closing, filled=len(before), riders=len(riders),
        )

    tile = per_passage((span, width), first)
    chunk = pl.BlockSpec((1, span, columns), lambda i, *_: (i + first, 0, part))
    if final:
        outs = [jax.ShapeDtypeStruct((passages, block, width), BF)] * pieces
        out_specs = [per_passage((block, width), first)] * pieces
    else:
        outs = [jax.ShapeDtypeStruct((count, span, width), F32)]
        out_specs = [per_passage((span, width))]
    outs.append(jax.ShapeDtypeStruct((2, columns), F32))
    out_specs.append(whole((2, columns)))
    if closing:
        outs += [jax.ShapeDtypeStruct((tall // 2, 3 * columns), F32)] * 2
        out_specs += [ANYWHERE] * 2
    else:
        outs.append(jax.ShapeDtypeStruct((tall, 3 * columns), F32))
        out_specs.append(ANYWHERE)
    operands = [x, q, k, v, lse, grad_mixed, grad_in, *weights]
    specs = [tile, chunk, chunk, chunk, per_passage(lse.shape[1:], first), chunk]
    specs.append(per_passage((span, width), grad_first))
    specs += [pl.BlockSpec((width, columns), lambda i, *_: (0, part))] * 3
    if total is not None:
        operands.append(total)
        specs.append(ANYWHERE)
    pairs = {}
    for i, value in enumerate(before):
        pairs[3 + len(operands)] = i
        operands.append(value)
        specs.append(ANYWHERE)
    pairs.update(alias(operands, specs, outs, out_specs, riders, 3))
    return pl.pallas_call(
        kernel,
        out_shape=outs,
        grid_spec=pltpu.PrefetchScalarGridSpec(
            num_scalar_prefetch=3,
            grid=(count,),
            in_specs=specs,
            out_specs=out_specs,
            scratch_shapes=[pltpu.VMEM((tall, 3 * columns), F32)]
            + [pltpu.VMEM((span, columns), BF)] * 3
            + [pltpu.VMEM((span, width), BF), pltpu.SemaphoreType.DMA((2,))],
        ),
        input_output_aliases=pairs,
        compiler_params=pltpu.CompilerParams(vmem_limit_bytes=VMEM_BYTES),
        cost_estimate=BRIEF,
    )(lens, src, core, *operands)


def tick(values):
    operands, specs, outs, out_specs = [], [], [], []
    pairs = alias(operands, specs, outs, out_specs, values, 0)
    return pl.pallas_call(
        lambda *refs: None,
        out_shape=outs,
        in_specs=specs,
        out_specs=out_specs,
        input_output_aliases=pairs,
        cost_estimate=TICK,
    )(*operands)


def flip(value, amount, axes, devices):
    return lax.ppermute(value, axes, [(i, i ^ amount) for i in range(devices)])


class Summing:
    def __init__(self, kept, sent, bits, short, me, devices, plan=(), extra=None):
        self.kept, self.sent, self.bits, self.short = kept, sent, list(bits), short
        self.me, self.devices, self.plan, self.extra = me, devices, list(plan), extra
        self.left = 0
        self.done = False

    def launch(self):
        bit = self.bits.pop(0)
        self.narrow = bit in self.short
        sent = self.sent.astype(BF) if self.narrow else self.sent
        if self.extra is not None:
            if self.narrow:
                high = lax.reduce_precision(self.extra, 8, 7)
                low = lax.reduce_precision(self.extra - high, 8, 7)
                self.extra = high + low
                sent = jnp.concatenate([sent, high.astype(BF), low.astype(BF)], axis=0)
            else:
                sent = jnp.concatenate([sent, self.extra], axis=0)
        self.came = flip(sent, 1 << bit, BOTH, self.devices)
        self.left = self.plan.pop(0) if self.plan else 1

    def land(self):
        self.left = 0
        rows = self.kept.shape[0]
        came = self.came.astype(F32)
        if self.extra is not None:
            n = self.extra.shape[0]
            more = came[rows : rows + n]
            if self.narrow:
                more = more + came[rows + n :]
            self.extra = self.extra + more
            came = came[:rows]
        value = self.kept + came
        if not self.bits:
            self.kept = value.astype(BF)
            self.done = True
            return
        side = (self.me >> self.bits[0]) & 1
        self.sent = lax.dynamic_slice_in_dim(value, (1 - side) * (rows // 2), rows // 2)
        self.kept = lax.dynamic_slice_in_dim(value, side * (rows // 2), rows // 2)


class Gathering:
    def __init__(self, value, bits, me, devices):
        self.kept, self.bits, self.me, self.devices = value, list(bits)[::-1], me, devices
        self.left = 0
        self.done = not self.bits

    def launch(self):
        self.bit = self.bits.pop(0)
        self.came = flip(self.kept, 1 << self.bit, BOTH, self.devices)
        self.left = 1

    def land(self):
        self.kept = jnp.where(
            ((self.me >> self.bit) & 1) == 0,
            jnp.concatenate([self.kept, self.came], axis=0),
            jnp.concatenate([self.came, self.kept], axis=0),
        )
        self.left = 0
        self.done = not self.bits


class Homing:
    def __init__(self, pieces, kind, seq_at, stretch):
        n = len(pieces)
        mine, block, width = pieces[0].shape
        self.kind, self.seq_at, self.stretch = kind, seq_at, stretch
        self.kept = jnp.zeros((n, mine, block, width), kind)
        self.waiting = [(k, pieces[k]) for k in (*range(2, n), 1)[: n - 1]]
        self.place(0, pieces[0])
        self.came = []
        self.left = 0
        self.done = False
        self.n = n

    def place(self, k, piece):
        self.kept = lax.dynamic_update_slice_in_dim(
            self.kept, piece.astype(self.kind)[None], self.seq_at ^ k, 0
        )

    def launch(self):
        take = max(1, (self.n - 1) // 3)
        self.came = [(k, flip(p, k, "seq", self.n)) for k, p in self.waiting[:take]]
        self.waiting = self.waiting[take:]
        self.left = self.stretch

    def land(self):
        for k, piece in self.came:
            self.place(k, piece)
        self.left = 0
        self.done = not self.waiting

    def whole(self):
        n, mine, block, width = self.kept.shape
        return self.kept.reshape(n * mine, block, width)


def in_order(every, bits):
    n = len(bits)
    width = every.shape[-1]
    every = every.reshape((2,) * n + (-1, width))
    every = every.transpose(tuple(n - 1 - b for b in bits) + (n, n + 1))
    return every.reshape(-1, width)


def local(
    tokens, sources, lengths, pairing, queries, w_query, b_query, w_key, w_value, b_value, w_out,
    b_out, gain_one, shift_one, w_up, b_up, w_down, second_feedforward_offset, gain_two, shift_two,
):
    documents, block, width = tokens.shape
    n_seq, n_dp = lax.axis_size("seq"), lax.axis_size("dp")
    devices = n_seq * n_dp
    seq_at, dp_at = lax.axis_index("seq"), lax.axis_index("dp")
    me = dp_at * n_seq + seq_at
    mine = documents // n_seq
    batch = documents * n_dp
    units = w_up.shape[1]
    src = seq_at ^ jnp.arange(n_seq, dtype=jnp.int32)
    lens = lax.dynamic_slice_in_dim(lengths, seq_at * mine, mine)

    def arriving(first, count, before):
        late = 0
        if before is not None:
            late = (before[-1][0, 0, 0] != before[-1][0, 0, 0]).astype(jnp.int32)
        pieces = []
        for k in range(n_seq):
            rows = lax.dynamic_slice_in_dim(tokens, (seq_at ^ k) * mine + first + late, count)
            pieces.append(rows if k == 0 else flip(rows, k, "seq", n_seq))
        return pieces

    weights = (w_query, w_key, w_value, w_out, w_up, w_down)
    row = lambda v: v[None, :]
    vectors = [b_query, b_value, b_out, gain_one, shift_one, second_feedforward_offset, gain_two,
               shift_two, b_up]
    vectors = jnp.concatenate(vectors).reshape(-1, width)
    saved = None
    first = 0
    pieces = None
    dp_hops = n_dp.bit_length() - 1
    hop = lambda value, bit: flip(value, 1 << bit, "dp", n_dp)
    spread = queries[None]
    done = min(1, dp_hops)
    if done:
        spread = jnp.concatenate([spread, hop(spread, 0)], axis=0)
    for count in (1, mine - 1):
        pieces = arriving(first, count, pieces)
        came = [hop(spread, done)] if done < dp_hops else []
        *saved, spread = forward(
            lens, src, pieces, weights, vectors, mine, first, saved, (spread,)
        )
        spread = jnp.concatenate([spread] + came, axis=0)
        done += len(came)
        first += count
    for bit in range(done, dp_hops):
        spread = jnp.concatenate([spread, hop(spread, bit)], axis=0)
    (x, q, k, v, mixed, lse, unit_one, inverse_one, hidden_low, gelu, slope, unit_two, inverse_two,
     unit_sums) = saved[:14]
    act = saved[14:]

    asked = jnp.concatenate(
        [lax.dynamic_index_in_dim(spread, dp_at ^ i, 0, False) for i in range(n_dp)], axis=0
    ).astype(F32)
    asked = asked * lax.rsqrt(jnp.sum(asked * asked, axis=-1, keepdims=True) + 1e-06)
    count = lens.astype(F32)[:, None]
    pooled = (unit_sums[:, 0, :] * gain_two + count * shift_two) / count
    pooled_inverse = lax.rsqrt(jnp.sum(pooled * pooled, axis=-1, keepdims=True) + 1e-06)
    pooled_unit = pooled * pooled_inverse
    own = jnp.dot(pooled_unit, asked.T, precision=EXACT) / TEMPERATURE
    scores = own[None]
    for bit in range(devices.bit_length() - 1):
        scores = jnp.concatenate([scores, flip(scores, 1 << bit, BOTH, devices)], axis=0)
    scores = scores.reshape(batch, batch)
    everyone = jnp.arange(batch, dtype=jnp.int32)
    order = ((me ^ jnp.arange(devices, dtype=jnp.int32))[:, None] * mine
             + jnp.arange(mine, dtype=jnp.int32)[None, :]).reshape(batch)
    pick = lambda index: jnp.sum(
        jnp.where(index[:, None] == everyone[None, :], sources[None, :], 0), axis=1
    )
    same = pick(order)[:, None] == pick(pairing)[None, :]
    match = order[:, None] == pairing[None, :]
    scores = jnp.where(same, scores, MASKED)
    top = jnp.max(scores, axis=0)
    log_total = top + jnp.log(jnp.sum(jnp.exp(scores - top), axis=0))
    chosen = jnp.sum(jnp.where(match, scores, 0.0), axis=0)
    loss = jnp.sum(log_total - chosen) / batch
    grad_scores = (jnp.exp(scores[:mine] - log_total) - match[:mine].astype(F32)) * (
        1.0 / batch / TEMPERATURE
    )
    grad_unit = jnp.dot(grad_scores, asked, precision=EXACT)
    grad_pooled = pooled_inverse * (
        grad_unit - pooled_unit * jnp.sum(grad_unit * pooled_unit, axis=-1, keepdims=True)
    )
    each = grad_pooled / count
    push = (each * gain_two)[:, None, :]
    grad_gain_two = jnp.sum(each * unit_sums[:, 0, :], axis=0)
    grad_shift_two = jnp.sum(grad_pooled, axis=0)

    seq_bits = n_seq.bit_length() - 1
    top_bit = devices.bit_length() - 1
    far_bits = tuple(range(seq_bits + 1, top_bit))
    bits = (0, seq_bits) + tuple(range(1, seq_bits)) + far_bits
    bits_b = tuple(range(top_bit))
    short = range(1, seq_bits + 1)
    core = (me & 1)[None]
    feed_parts = units // width
    heads_parts = 1
    feed = (gelu, slope, hidden_low, w_down, w_up, w_out)
    flying = []

    def begin(kept, sent, bits, *plan, extra=None):
        one = Summing(kept, sent, bits, short, me, devices, plan, extra)
        flying.append(one)
        return one

    def riding():
        for one in flying:
            if not one.left and not one.done:
                one.launch()
        return tuple(one.kept for one in flying)

    def landing(kept):
        for one, value in zip(list(flying), kept):
            one.kept = value
            if one.done:
                flying.remove(one)
                continue
            one.left -= 1
            if not one.left:
                one.land()

    up_biases = []
    operands = (push, unit_two, inverse_two)
    chunks = []
    for part in range(feed_parts):
        closing = part == feed_parts - 1
        second = part % 2
        if closing:
            operands = operands + (unit_one, inverse_one, mixed, row(gain_one))
        riders = riding()
        if part == 0:
            riders += tuple(act)
        tall_all = 2 * width + (width // 2 if part >= feed_parts - 2 else 0)
        grad_hidden, low, up_bias, rows, kept, sent, *landed = feed_back(
            lens, core, operands, *feed, part, feed_parts, second * width, tall_all,
            (kept, sent) if second else None, riders,
        )
        if part == 0:
            activations = Homing(landed, BF, seq_at, 1)
            activations.waiting.sort()
            flying.append(activations)
        else:
            landing(landed)
        up_biases.append(up_bias)
        if part == 0:
            rows_a, grad_low = rows, low
        operands = (grad_low, grad_hidden)
        if second:
            chunks.append(begin(kept, sent, *((bits_b, 1, 2) if closing else (bits,))))
    grad_one, grad_mixed, rows_b = grad_hidden, low, rows
    biases = []
    grad_in = grad_one
    for part in range(heads_parts):
        riders = riding()
        outs = attention_back(
            lens, src, core, n_seq, x, q, k, v, lse, grad_mixed, grad_in,
            (w_query, w_key, w_value), part, heads_parts, 0, mine, 0, None, True, (), riders,
        )
        n = n_seq if part == heads_parts - 1 else 1
        landing(outs[n + 3 :])
        grad_in = outs[0]
        biases.append(outs[n])
        kept, sent = outs[n + 1 : n + 3]
        extra = None
        if part == heads_parts - 1:
            extra = jnp.concatenate(
                [
                    jnp.concatenate(biases, axis=1), rows_b[0:3], rows_a[3:4],
                    row(grad_gain_two), row(grad_shift_two),
                    jnp.concatenate(up_biases, axis=1).reshape(feed_parts, width),
                    jnp.zeros((-(8 + feed_parts) % 16, width), F32),
                ],
                axis=0,
            )
        extra = jnp.concatenate([extra, jnp.zeros((-len(extra) % 3, width), F32)], axis=0)
        chunks.append(begin(kept, sent, bits, extra=extra.reshape(-1, 3 * width)))
    homes = Homing(outs[:n_seq], F32, seq_at, 2)
    flying.append(homes)
    first, second, heads = chunks
    feed = attention = None
    while flying:
        if first.done and second.done and feed is None:
            feed = jnp.concatenate([first.kept, second.kept], axis=0)
            feed = lax.all_gather(feed, BOTH, axis=0)
        if heads.done and attention is None:
            attention = Gathering(heads.kept, bits, me, devices)
            flying.append(attention)
        flying = [one for one in flying if not one.done]
        if flying:
            landing(tick(riding()))
    small = heads.extra.reshape(-1, width)
    attention = attention.kept
    cut = first.kept.shape[0]
    all_a, all_b = in_order(feed[:, :cut], bits), in_order(feed[:, cut:], bits_b)
    activations, grad_tokens = activations.whole(), homes.whole()
    grads = [attention[:, n * width : (n + 1) * width].astype(F32) for n in range(3)]
    two = 2 * width
    half = two + width // 2
    again = half + width
    grad_down = jnp.concatenate([all_a[:two], all_b[:two]], axis=0).astype(F32)
    grad_out = jnp.concatenate(
        [all_b[two:half], all_b[again : again + width // 2]], axis=0
    ).astype(F32)
    grad_up = jnp.concatenate(
        [all_a[two : two + width], all_a[two + width :], all_b[half:again],
         all_b[again + width // 2 :]],
        axis=1,
    ).astype(F32)
    return (
        loss,
        activations,
        grad_tokens,
        grads[0],
        small[0],
        grads[1],
        grads[2],
        small[1],
        grad_out,
        small[4],
        small[2],
        small[3],
        grad_up,
        small[8 : 8 + feed_parts].reshape(units),
        grad_down,
        small[5],
        small[6],
        small[7],
    )


def solution(mesh):
    in_specs = (P("dp", "seq", None), P(), P("dp"), P(), P("dp", None)) + (P(),) * 15
    out_specs = (P(), P("dp", "seq", None), P("dp", "seq", None)) + (P(),) * 15
    return jax.shard_map(local, mesh=mesh, in_specs=in_specs, out_specs=out_specs, check_vma=False)
```

```python
import jax
import jax.numpy as jnp
from jax import lax
from jax.experimental import pallas as pl
from jax.experimental.pallas import tpu as pltpu
from jax.sharding import PartitionSpec as P

HEADS = 12
EPS = 1e-05
TEMPERATURE = 0.01
MASKED = -1000000000.0
SEQ = ("x", "core")
DP = ("far", "near")
BOTH = DP + SEQ
NEAR = ("near", "x")
FAR = ("far",)
EXACT = lax.Precision.HIGHEST
BF = jnp.bfloat16
F32 = jnp.float32
VMEM_BYTES = 60 * 2**20
BRIEF = pl.CostEstimate(flops=7 * 10**10, bytes_accessed=10**6, transcendentals=0)
TICK = pl.CostEstimate(flops=3 * 10**10, bytes_accessed=10**6, transcendentals=0)


def dot(left, right, left_at=1, right_at=0):
    return lax.dot_general(
        left, right, (((left_at,), (right_at,)), ((), ())), preferred_element_type=F32
    )


def normalize(value):
    centred = value - jnp.mean(value, axis=-1, keepdims=True)
    inverse = lax.rsqrt(jnp.mean(centred * centred, axis=-1, keepdims=True) + EPS)
    return centred * inverse, inverse


def norm_back(grad_unit, unit, inverse):
    first = jnp.mean(grad_unit, axis=-1, keepdims=True)
    second = jnp.mean(grad_unit * unit, axis=-1, keepdims=True)
    return inverse * (grad_unit - first - unit * second)


def gelu_and_slope(value):
    size = jnp.abs(value)
    t = 1.0 / (1.0 + (0.3275911 * 0.7071067811865476) * size)
    bell = jnp.exp(-0.5 * (value * value))
    tail = (
        (((0.5 * 1.061405429 * t - 0.5 * 1.453152027) * t + 0.5 * 1.421413741) * t
         - 0.5 * 0.284496736) * t + 0.5 * 0.254829592
    ) * t * bell
    below = jnp.where(value >= 0.0, 1.0 - tail, tail)
    return value * below, below + value * (bell * 0.3989422804014327)


def lane_half(width, which):
    lanes = lax.broadcasted_iota(jnp.int32, (1, width), 1)
    return ((lanes >= which * (width // 2)) & (lanes < (which + 1) * (width // 2))).astype(F32)


def whole(shape):
    return pl.BlockSpec(shape, lambda i, *_: (0,) * len(shape))


def per_passage(shape, first=0):
    return pl.BlockSpec((1,) + tuple(shape), lambda i, *_: (i + first,) + (0,) * len(shape))


ANYWHERE = pl.BlockSpec(memory_space=pl.ANY)


def fetch(sources, targets, sems):
    return [
        pltpu.make_async_copy(s, t, sems.at[i]) for i, (s, t) in enumerate(zip(sources, targets))
    ]


def forward_kernel(lens, src, *refs, pieces, first, aliased, riders):
    refs = list(refs)
    take = lambda n: [refs.pop(0) for _ in range(n)]
    x_in = take(pieces)
    hbm = take(6)
    (vectors,) = take(1)
    take(aliased + riders)
    (x_all, q_out, k_out, v_out, mixed_out, lse_out, unit_one_out, inverse_one_out,
     hidden_low_out, gelu_out, slope_out, unit_two_out, inverse_two_out, sums_out) = take(14)
    act = take(pieces)
    take(riders)
    held = take(6)
    act_held, sems = take(2)
    w_query, w_key, w_value, w_out, w_up, w_down = held
    b_query, b_value, b_out, gain_one, shift_one, b_down, gain_two, shift_two = (
        vectors[n : n + 1, :] for n in range(8)
    )
    step = pl.program_id(0)
    copies = fetch(hbm, held, sems)

    @pl.when(step == 0)
    def _():
        for copy in copies:
            copy.start()

    def ready(*which):
        @pl.when(step == 0)
        def _():
            for i in which:
                copies[i].wait()

    span, width = x_all.shape[1:]
    block = span // pieces
    head = width // HEADS
    pair = 2 * head
    length = lens[first + step]
    for k in range(pieces):
        x_all[0, pl.ds(pl.multiple_of(src[k] * block, block), block), :] = x_in[k][0]
    x = x_all[0]
    ready(0, 1, 2)
    q_out[0] = ((dot(x, w_query[...]) + b_query) * (head ** -0.5)).astype(BF)
    k_out[0] = dot(x, w_key[...]).astype(BF)
    v_out[0] = (dot(x, w_value[...]) + b_value).astype(BF)
    key_mask = jnp.where(
        lax.broadcasted_iota(jnp.int32, (1, span), 1) < length, 0.0, MASKED
    ).astype(F32)
    lanes = lax.broadcasted_iota(jnp.int32, (1, 128), 1)
    stats = jnp.zeros((span, 128), F32)
    for p in range(HEADS // 2):
        at = slice(p * pair, (p + 1) * pair)
        qp, kp, vp = q_out[0, :, at], k_out[0, :, at], v_out[0, :, at]
        total = None
        for h in range(2):
            half = lane_half(pair, h).astype(BF)
            scores = dot(qp, kp * half, 1, 1) + key_mask
            top = jnp.max(scores, axis=-1, keepdims=True)
            expo = jnp.exp(scores - top)
            norm = jnp.sum(expo, axis=-1, keepdims=True)
            low = (expo * (1.0 / norm)).astype(BF)
            term = dot(low, vp * half)
            total = term if total is None else total + term
            stats = jnp.where(lanes == 2 * p + h, top + jnp.log(norm), stats)
        mixed_out[0, :, at] = total.astype(BF)
    lse_out[0] = stats.T[: lse_out.shape[1]]
    ready(3)
    unit_one, inverse_one = normalize(x.astype(F32) + (dot(mixed_out[0], w_out[...]) + b_out))
    unit_one_out[0] = unit_one.astype(BF)
    inverse_one_out[0] = inverse_one
    hidden = unit_one * gain_one + shift_one
    hidden_low = hidden.astype(BF)
    hidden_low_out[0] = hidden_low
    ready(4, 5)
    total = hidden + b_down
    for c in range(gelu_out.shape[2] // width):
        at = slice(c * width, (c + 1) * width)
        value, slope = gelu_and_slope(dot(hidden_low, w_up[:, at]) + vectors[8 + c : 9 + c, :])
        low = value.astype(BF)
        gelu_out[0, :, at] = low
        slope_out[0, :, at] = slope.astype(BF)
        total = total + dot(low, w_down[at, :])
    unit_two, inverse_two = normalize(total)
    unit_two_out[0] = unit_two.astype(BF)
    inverse_two_out[0] = inverse_two
    act_held[...] = (unit_two * gain_two + shift_two).astype(BF)
    for k in range(pieces):
        act[k][0] = act_held[pl.ds(pl.multiple_of(src[k] * block, block), block), :]
    live = (lax.broadcasted_iota(jnp.int32, (span, 1), 0) < length).astype(F32)
    sums_out[0] = jnp.sum(unit_two * live, axis=0, keepdims=True)


def forward(lens, src, pieces, weights, vectors, passages, first, before, riders):
    count, block, width = pieces[0].shape
    n = len(pieces)
    span = block * n
    units = weights[4].shape[1]
    shapes = [
        ((span, width), BF), ((span, width), BF), ((span, width), BF), ((span, width), BF),
        ((span, width), BF), ((16, span), F32), ((span, width), BF), ((span, 1), F32),
        ((span, width), BF), ((span, units), BF), ((span, units), BF), ((span, width), BF),
        ((span, 1), F32), ((1, width), F32),
    ]
    outs = [jax.ShapeDtypeStruct((passages,) + s, t) for s, t in shapes]
    outs += [jax.ShapeDtypeStruct((passages, block, width), BF)] * n
    out_specs = [per_passage(o.shape[1:], first) for o in outs]
    kinds = len(outs)
    in_specs = [per_passage((block, width))] * n + [ANYWHERE] * 6 + [whole(vectors.shape)]
    operands = list(pieces) + list(weights) + [vectors]
    aliases = {}
    if before is not None:
        for i, value in enumerate(before):
            aliases[2 + len(operands)] = i
            operands.append(value)
            in_specs.append(ANYWHERE)
    aliases.update(alias(operands, in_specs, outs, out_specs, riders, 2))

    def kernel(*refs):
        forward_kernel(
            *refs, pieces=n, first=first, aliased=0 if before is None else kinds,
            riders=len(riders),
        )

    return pl.pallas_call(
        kernel,
        out_shape=outs,
        grid_spec=pltpu.PrefetchScalarGridSpec(
            num_scalar_prefetch=2,
            grid=(count,),
            in_specs=in_specs,
            out_specs=out_specs,
            scratch_shapes=[pltpu.VMEM(w.shape, BF) for w in weights]
            + [pltpu.VMEM((span, width), BF), pltpu.SemaphoreType.DMA((6,))],
        ),
        input_output_aliases=aliases,
        compiler_params=pltpu.CompilerParams(vmem_limit_bytes=VMEM_BYTES),
        cost_estimate=BRIEF,
    )(lens, src, *operands)


def second_norm_back(length, push, unit_two, inverse_two):
    live = lax.broadcasted_iota(jnp.int32, (unit_two.shape[0], 1), 0) < length
    return jnp.where(live, norm_back(push, unit_two, inverse_two), 0.0)


def hand_over(total, kept_hbm, sent_hbm, side, row, column, sems):
    half, columns = total.shape[0] // 2, total.shape[1]
    own = pl.multiple_of(side * half, half)
    other = pl.multiple_of((1 - side) * half, half)
    copies = [
        pltpu.make_async_copy(
            total.at[pl.ds(at, half), :],
            out.at[pl.ds(row, half), pl.ds(column, columns)],
            sem,
        )
        for at, out, sem in ((own, kept_hbm, sems.at[0]), (other, sent_hbm, sems.at[1]))
    ]
    for copy in copies:
        copy.start()
    for copy in copies:
        copy.wait()


def alias(operands, specs, outs, out_specs, values, offset):
    pairs = {}
    for value in values:
        pairs[offset + len(operands)] = len(outs)
        operands.append(value)
        specs.append(ANYWHERE)
        outs.append(jax.ShapeDtypeStruct(value.shape, value.dtype))
        out_specs.append(ANYWHERE)
    return pairs


def feed_kernel(lens, core, *refs, part, parts, place, filling, riders):
    refs = list(refs)
    take = lambda n: [refs.pop(0) for _ in range(n)]
    opening, closing = part == 0, part == parts - 1
    if opening:
        push, unit_two, inverse_two = take(3)
    else:
        grad_low_in, grad_hidden_in = take(2)
    if closing:
        unit_one, inverse_one, mixed, gain_one = take(4)
    gelu, slope, hidden_low, w_down, w_up = take(5)
    if closing:
        (w_out,) = take(1)
    take((2 if filling else 0) + riders)
    grad_hidden_out, low_out, up_bias, rows = take(4)
    kept_hbm, sent_hbm = take(2)
    take(riders)
    total, sems = take(2)
    step = pl.program_id(0)
    last = pl.num_programs(0) - 1
    units, width = w_down.shape

    @pl.when(step == 0)
    def _():
        total[...] = jnp.zeros_like(total)
        up_bias[...] = jnp.zeros_like(up_bias)
        rows[...] = jnp.zeros_like(rows)

    if opening:
        grad_hidden = second_norm_back(
            lens[step], push[0], unit_two[0].astype(F32), inverse_two[0]
        )
        grad_low = grad_hidden.astype(BF)
        low_out[0] = grad_low
        rows[3:4, :] += jnp.sum(grad_low.astype(F32), axis=0, keepdims=True)
    else:
        grad_hidden = grad_hidden_in[0]
        grad_low = grad_low_in[0]
    up_low = (dot(grad_low, w_down[...], 1, 1) * slope[0].astype(F32)).astype(BF)
    total[:units, :] += dot(gelu[0], grad_low, 0, 0)
    up_bias[...] += jnp.sum(up_low.astype(F32), axis=0, keepdims=True)
    total[total.shape[0] - width :, :] += dot(hidden_low[0], up_low, 0, 0)
    grad_hidden = grad_hidden + dot(up_low, w_up[...], 1, 1)
    if closing:
        unit = unit_one[0].astype(F32)
        rows[0:1, :] += jnp.sum(grad_hidden * unit, axis=0, keepdims=True)
        rows[1:2, :] += jnp.sum(grad_hidden, axis=0, keepdims=True)
        grad_one = norm_back(grad_hidden * gain_one[...], unit, inverse_one[0])
        grad_hidden_out[0] = grad_one
        branch_low = grad_one.astype(BF)
        rows[2:3, :] += jnp.sum(branch_low.astype(F32), axis=0, keepdims=True)
        total[units : units + width, :] += dot(mixed[0], branch_low, 0, 0)
        low_out[0] = dot(branch_low, w_out[...], 1, 1).astype(BF)
    else:
        grad_hidden_out[0] = grad_hidden

    @pl.when(step == last)
    def _():
        hand_over(total, kept_hbm, sent_hbm, core[0], place, 0, sems)


def feed_back(lens, core, row_operands, gelu, slope, hidden_low, w_down, w_up, w_out, part, parts,
              place, tall_all, filled, riders):
    opening, closing = part == 0, part == parts - 1
    passages, span, units = gelu.shape
    units //= parts
    width = w_down.shape[1]
    tall = 2 * units + (width if closing else 0)
    tile = per_passage((span, width))
    column = per_passage((span, 1))
    chunk = pl.BlockSpec((1, span, units), lambda i, *_: (i, 0, part))
    specs = [per_passage((1, width)), tile, column] if opening else [tile, tile]
    operands = list(row_operands)
    if closing:
        specs += [tile, column, tile, whole((1, width))]
    operands += [gelu, slope, hidden_low, w_down, w_up]
    specs += [
        chunk, chunk, tile,
        pl.BlockSpec((units, width), lambda i, *_: (part, 0)),
        pl.BlockSpec((width, units), lambda i, *_: (0, part)),
    ]
    if closing:
        operands.append(w_out)
        specs.append(whole((width, width)))
    like = lambda t: jax.ShapeDtypeStruct((passages, span, width), t)
    outs = [
        like(F32), like(BF), jax.ShapeDtypeStruct((1, units), F32),
        jax.ShapeDtypeStruct((8, width), F32),
    ]
    out_specs = [tile, tile, whole((1, units)), whole((8, width))]
    if filled is None:
        outs += [jax.ShapeDtypeStruct((tall_all, width), F32)] * 2
        out_specs += [ANYWHERE] * 2
        pairs = alias(operands, specs, outs, out_specs, riders, 2)
    else:
        pairs = alias(operands, specs, outs, out_specs, tuple(filled) + tuple(riders), 2)

    def kernel(*refs):
        feed_kernel(
            *refs, part=part, parts=parts, place=place, filling=filled is not None,
            riders=len(riders),
        )

    return pl.pallas_call(
        kernel,
        out_shape=outs,
        grid_spec=pltpu.PrefetchScalarGridSpec(
            num_scalar_prefetch=2,
            grid=(passages,),
            in_specs=specs,
            out_specs=out_specs,
            scratch_shapes=[pltpu.VMEM((tall, width), F32), pltpu.SemaphoreType.DMA((2,))],
        ),
        input_output_aliases=pairs,
        compiler_params=pltpu.CompilerParams(vmem_limit_bytes=VMEM_BYTES),
        cost_estimate=BRIEF,
    )(lens, core, *operands)


def attention_kernel(
    lens, src, core, *refs, pieces, final, part, first, opening, closing, filled, riders
):
    refs = list(refs)
    take = lambda n: [refs.pop(0) for _ in range(n)]
    x, q, k, v, lse, grad_mixed, grad_in = take(7)
    weights = take(3)
    if not opening:
        (total_in,) = take(1)
    take(filled + riders)
    out = take(pieces if final else 1)
    (bias,) = take(1)
    totals_out = take(2 if closing else 1)
    take(riders)
    total = take(1)[0]
    lows = take(3)
    tokens_low, sems = take(2)
    step = pl.program_id(0)
    last = pl.num_programs(0) - 1
    span, columns = q.shape[1:]
    width = x.shape[2]
    block = span // pieces
    head = width // HEADS
    pair = 2 * head
    scale = head ** -0.5
    if not opening:
        before = pltpu.make_async_copy(total_in, total, sems.at[0])

    @pl.when(step == 0)
    def _():
        if opening:
            total[...] = jnp.zeros_like(total)
        else:
            before.start()
        bias[...] = jnp.zeros_like(bias)

    key_mask = jnp.where(
        lax.broadcasted_iota(jnp.int32, (span, 1), 0) < lens[first + step], 0.0, MASKED
    ).astype(F32)
    query_low, key_low, value_low = lows
    for p in range(columns // pair):
        at = slice(p * pair, (p + 1) * pair)
        qp, kp, vp, gp = q[0, :, at], k[0, :, at], v[0, :, at], grad_mixed[0, :, at]
        gq = gk = gv = None
        for h in range(2):
            half = lane_half(pair, h).astype(BF)
            qm, gm, km = qp * half, gp * half, kp * half
            n = part * (columns // head) + 2 * p + h
            probs = jnp.exp((dot(kp, qm, 1, 1) + key_mask) - lse[0, n : n + 1, :])
            low = probs.astype(BF)
            grad_probs = dot(vp, gm, 1, 1)
            delta = jnp.sum(probs * grad_probs, axis=0, keepdims=True)
            scores = (probs * (grad_probs - delta)).astype(BF)
            tv = dot(low, gm)
            tk = dot(scores, qm)
            tq = dot(scores, km, 0, 0)
            gv = tv if gv is None else gv + tv
            gk = tk if gk is None else gk + tk
            gq = tq if gq is None else gq + tq
        query_low[:, at] = (gq * scale).astype(BF)
        key_low[:, at] = gk.astype(BF)
        value_low[:, at] = gv.astype(BF)

    if not opening:

        @pl.when(step == 0)
        def _():
            before.wait()

    grad = grad_in[0]
    for n, (low, weight) in enumerate(zip(lows, weights)):
        grad = grad + dot(low[...], weight[...], 1, 1)
        total[:, n * columns : (n + 1) * columns] += dot(x[0], low[...], 0, 0)
    bias[0:1, :] += jnp.sum(query_low[...].astype(F32), axis=0, keepdims=True)
    bias[1:2, :] += jnp.sum(value_low[...].astype(F32), axis=0, keepdims=True)
    if final:
        tokens_low[...] = grad.astype(BF)
        for n in range(pieces):
            out[n][0] = tokens_low[pl.ds(pl.multiple_of(src[n] * block, block), block), :]
    else:
        out[0][0] = grad

    @pl.when(step == last)
    def _():
        if closing:
            hand_over(total, *totals_out, core[0], 0, 0, sems)
        else:
            after = pltpu.make_async_copy(total, totals_out[0], sems.at[1])
            after.start()
            after.wait()


def attention_back(lens, src, core, pieces, x, q, k, v, lse, grad_mixed, grad_in, weights, part,
                   parts, first, count, grad_first, total, closing, before, riders):
    passages, span, width = x.shape
    block = span // pieces
    columns = width // parts
    final = part == parts - 1
    tall = width

    def kernel(*refs):
        attention_kernel(
            *refs, pieces=pieces, final=final, part=part, first=first, opening=total is None,
            closing=closing, filled=len(before), riders=len(riders),
        )

    tile = per_passage((span, width), first)
    chunk = pl.BlockSpec((1, span, columns), lambda i, *_: (i + first, 0, part))
    if final:
        outs = [jax.ShapeDtypeStruct((passages, block, width), BF)] * pieces
        out_specs = [per_passage((block, width), first)] * pieces
    else:
        outs = [jax.ShapeDtypeStruct((count, span, width), F32)]
        out_specs = [per_passage((span, width))]
    outs.append(jax.ShapeDtypeStruct((2, columns), F32))
    out_specs.append(whole((2, columns)))
    if closing:
        outs += [jax.ShapeDtypeStruct((tall // 2, 3 * columns), F32)] * 2
        out_specs += [ANYWHERE] * 2
    else:
        outs.append(jax.ShapeDtypeStruct((tall, 3 * columns), F32))
        out_specs.append(ANYWHERE)
    operands = [x, q, k, v, lse, grad_mixed, grad_in, *weights]
    specs = [tile, chunk, chunk, chunk, per_passage(lse.shape[1:], first), chunk]
    specs.append(per_passage((span, width), grad_first))
    specs += [pl.BlockSpec((width, columns), lambda i, *_: (0, part))] * 3
    if total is not None:
        operands.append(total)
        specs.append(ANYWHERE)
    pairs = {}
    for i, value in enumerate(before):
        pairs[3 + len(operands)] = i
        operands.append(value)
        specs.append(ANYWHERE)
    pairs.update(alias(operands, specs, outs, out_specs, riders, 3))
    return pl.pallas_call(
        kernel,
        out_shape=outs,
        grid_spec=pltpu.PrefetchScalarGridSpec(
            num_scalar_prefetch=3,
            grid=(count,),
            in_specs=specs,
            out_specs=out_specs,
            scratch_shapes=[pltpu.VMEM((tall, 3 * columns), F32)]
            + [pltpu.VMEM((span, columns), BF)] * 3
            + [pltpu.VMEM((span, width), BF), pltpu.SemaphoreType.DMA((2,))],
        ),
        input_output_aliases=pairs,
        compiler_params=pltpu.CompilerParams(vmem_limit_bytes=VMEM_BYTES),
        cost_estimate=BRIEF,
    )(lens, src, core, *operands)


def tick(values, cost):
    operands, specs, outs, out_specs = [], [], [], []
    pairs = alias(operands, specs, outs, out_specs, values, 0)
    return pl.pallas_call(
        lambda *refs: None,
        out_shape=outs,
        in_specs=specs,
        out_specs=out_specs,
        input_output_aliases=pairs,
        cost_estimate=cost,
    )(*operands)


def flip(value, amount, axes, devices):
    return lax.ppermute(value, axes, [(i, i ^ amount) for i in range(devices)])


def exchange(blocks, axes):
    return lax.all_to_all(blocks, axes, split_axis=0, concat_axis=0, tiled=True)


class Summing:
    def __init__(self, kept, sent, extra=None, narrow=(NEAR,), hops=False):
        self.kept, self.sent, self.extra = kept, sent, extra
        self.narrow, self.hops = narrow, hops
        self.stages = [None, NEAR, FAR]
        self.left = 0
        self.done = False
        self.apart = None

    def launch(self):
        self.axes = self.stages.pop(0)
        self.left = 1
        if self.axes is None:
            self.came = flip(self.sent, 1, BOTH, lax.axis_size(BOTH))
            if self.extra is not None:
                self.apart = flip(self.extra, 1, BOTH, lax.axis_size(BOTH))
            return
        n = lax.axis_size(self.axes)
        rows, width = self.kept.shape
        sent = self.value.reshape(n, rows, width)
        if self.axes is FAR and self.hops:
            at = lax.axis_index(FAR)
            self.came = [
                flip(lax.dynamic_index_in_dim(sent, at ^ k, 0, False), k, FAR, n)
                for k in range(1, n)
            ]
            self.left = 2
            return
        spread = lambda v: jnp.broadcast_to(v[None], (n,) + v.shape)
        more = []
        if self.axes in self.narrow:
            sent = sent.astype(BF)
            if self.extra is not None:
                high = lax.reduce_precision(self.extra, 8, 7)
                low = lax.reduce_precision(self.extra - high, 8, 7)
                self.extra = high + low
                more = [spread(high.astype(BF)), spread(low.astype(BF))]
        elif self.extra is not None:
            more = [spread(self.extra)]
        self.came = exchange(jnp.concatenate([sent] + more, axis=1) if more else sent, self.axes)

    def land(self):
        rows = self.kept.shape[0]
        if isinstance(self.came, list):
            self.kept = sum(self.came, self.kept).astype(BF)
            self.left, self.done = 0, True
            return
        came = self.came.astype(F32)
        if self.axes is None:
            value = self.kept + came
            if self.extra is not None:
                self.extra = self.extra + self.apart
        else:
            other = jnp.arange(came.shape[0]) != lax.axis_index(self.axes)
            value = self.kept + jnp.sum(
                jnp.where(other[:, None, None], came[:, :rows], 0.0), axis=0
            )
            if self.extra is not None:
                more = jnp.sum(came[:, rows:], axis=0)
                self.extra = jnp.sum(more.reshape((-1,) + self.extra.shape), axis=0)
        self.left = 0
        if not self.stages:
            self.kept = value.astype(BF)
            self.done = True
            return
        self.value = value
        part = value.shape[0] // lax.axis_size(self.stages[0])
        self.kept = lax.dynamic_slice_in_dim(
            value, lax.axis_index(self.stages[0]) * part, part
        )


class Gathering:
    def __init__(self, value):
        self.kept = value
        self.stages = [FAR, NEAR, None]
        self.left = 0
        self.done = False

    def launch(self):
        self.axes = self.stages.pop(0)
        self.left = 1
        if self.axes is None:
            self.came = flip(self.kept, 1, BOTH, lax.axis_size(BOTH))
        else:
            n = lax.axis_size(self.axes)
            self.came = exchange(
                jnp.broadcast_to(self.kept[None], (n,) + self.kept.shape), self.axes
            )

    def land(self):
        if self.axes is None:
            self.kept = jnp.where(
                lax.axis_index("core") == 0,
                jnp.concatenate([self.kept, self.came], axis=0),
                jnp.concatenate([self.came, self.kept], axis=0),
            )
        else:
            own = jnp.arange(self.came.shape[0]) == lax.axis_index(self.axes)
            self.kept = jnp.where(own[:, None, None], self.kept[None], self.came).reshape(
                -1, self.kept.shape[1]
            )
        self.left = 0
        self.done = not self.stages


class Homing:
    def __init__(self, pieces, kind, seq_at, stretch):
        n = len(pieces)
        mine, block, width = pieces[0].shape
        self.kind, self.seq_at, self.stretch = kind, seq_at, stretch
        self.kept = jnp.zeros((n, mine, block, width), kind)
        self.waiting = [(k, pieces[k]) for k in (*range(2, n), 1)[: n - 1]]
        self.place(0, pieces[0])
        self.came = []
        self.left = 0
        self.done = False
        self.n = n

    def place(self, k, piece):
        self.kept = lax.dynamic_update_slice_in_dim(
            self.kept, piece.astype(self.kind)[None], self.seq_at ^ k, 0
        )

    def launch(self):
        take = max(1, (self.n - 1) // 3)
        self.came = [(k, flip(p, k, SEQ, self.n)) for k, p in self.waiting[:take]]
        self.waiting = self.waiting[take:]
        self.left = self.stretch

    def land(self):
        for k, piece in self.came:
            self.place(k, piece)
        self.left = 0
        self.done = not self.waiting

    def whole(self):
        n, mine, block, width = self.kept.shape
        return self.kept.reshape(n * mine, block, width)


def in_order(every):
    n_far, n_near, n_x, n_core = (lax.axis_size(axis) for axis in BOTH)
    width = every.shape[1]
    every = every.reshape(n_far, n_near, n_x, n_core, -1, width)
    return every.transpose(3, 1, 2, 0, 4, 5).reshape(-1, width)


def local(
    tokens, sources, lengths, pairing, queries, w_query, b_query, w_key, w_value, b_value, w_out,
    b_out, gain_one, shift_one, w_up, b_up, w_down, second_feedforward_offset, gain_two, shift_two,
):
    documents, block, width = tokens.shape
    n_seq, n_dp = lax.axis_size(SEQ), lax.axis_size(DP)
    devices = n_seq * n_dp
    seq_at, dp_at = lax.axis_index(SEQ), lax.axis_index(DP)
    me = dp_at * n_seq + seq_at
    mine = documents // n_seq
    batch = documents * n_dp
    units = w_up.shape[1]
    src = seq_at ^ jnp.arange(n_seq, dtype=jnp.int32)
    lens = lax.dynamic_slice_in_dim(lengths, seq_at * mine, mine)

    def arriving(first, count, before):
        late = 0
        if before is not None:
            late = (before[-1][0, 0, 0] != before[-1][0, 0, 0]).astype(jnp.int32)
        pieces = []
        for k in range(n_seq):
            rows = lax.dynamic_slice_in_dim(tokens, (seq_at ^ k) * mine + first + late, count)
            pieces.append(rows if k == 0 else flip(rows, k, SEQ, n_seq))
        return pieces

    weights = (w_query, w_key, w_value, w_out, w_up, w_down)
    row = lambda v: v[None, :]
    vectors = [b_query, b_value, b_out, gain_one, shift_one, second_feedforward_offset, gain_two,
               shift_two, b_up]
    vectors = jnp.concatenate(vectors).reshape(-1, width)
    saved = None
    first = 0
    pieces = None
    dp_hops = n_dp.bit_length() - 1
    hop = lambda value, bit: flip(value, 1 << bit, DP, n_dp)
    spread = queries[None]
    done = min(1, dp_hops)
    if done:
        spread = jnp.concatenate([spread, hop(spread, 0)], axis=0)
    for count in (1, mine - 1):
        pieces = arriving(first, count, pieces)
        came = [hop(spread, done)] if done < dp_hops else []
        *saved, spread = forward(
            lens, src, pieces, weights, vectors, mine, first, saved, (spread,)
        )
        spread = jnp.concatenate([spread] + came, axis=0)
        done += len(came)
        first += count
    for bit in range(done, dp_hops):
        spread = jnp.concatenate([spread, hop(spread, bit)], axis=0)
    (x, q, k, v, mixed, lse, unit_one, inverse_one, hidden_low, gelu, slope, unit_two, inverse_two,
     unit_sums) = saved[:14]
    act = saved[14:]

    asked = jnp.concatenate(
        [lax.dynamic_index_in_dim(spread, dp_at ^ i, 0, False) for i in range(n_dp)], axis=0
    ).astype(F32)
    asked = asked * lax.rsqrt(jnp.sum(asked * asked, axis=-1, keepdims=True) + 1e-06)
    count = lens.astype(F32)[:, None]
    pooled = (unit_sums[:, 0, :] * gain_two + count * shift_two) / count
    pooled_inverse = lax.rsqrt(jnp.sum(pooled * pooled, axis=-1, keepdims=True) + 1e-06)
    pooled_unit = pooled * pooled_inverse
    own = jnp.dot(pooled_unit, asked.T, precision=EXACT) / TEMPERATURE
    scores = own[None]
    for bit in range(devices.bit_length() - 1):
        scores = jnp.concatenate([scores, flip(scores, 1 << bit, BOTH, devices)], axis=0)
    scores = scores.reshape(batch, batch)
    everyone = jnp.arange(batch, dtype=jnp.int32)
    order = ((me ^ jnp.arange(devices, dtype=jnp.int32))[:, None] * mine
             + jnp.arange(mine, dtype=jnp.int32)[None, :]).reshape(batch)
    pick = lambda index: jnp.sum(
        jnp.where(index[:, None] == everyone[None, :], sources[None, :], 0), axis=1
    )
    same = pick(order)[:, None] == pick(pairing)[None, :]
    match = order[:, None] == pairing[None, :]
    scores = jnp.where(same, scores, MASKED)
    top = jnp.max(scores, axis=0)
    log_total = top + jnp.log(jnp.sum(jnp.exp(scores - top), axis=0))
    chosen = jnp.sum(jnp.where(match, scores, 0.0), axis=0)
    loss = jnp.sum(log_total - chosen) / batch
    grad_scores = (jnp.exp(scores[:mine] - log_total) - match[:mine].astype(F32)) * (
        1.0 / batch / TEMPERATURE
    )
    grad_unit = jnp.dot(grad_scores, asked, precision=EXACT)
    grad_pooled = pooled_inverse * (
        grad_unit - pooled_unit * jnp.sum(grad_unit * pooled_unit, axis=-1, keepdims=True)
    )
    each = grad_pooled / count
    push = (each * gain_two)[:, None, :]
    grad_gain_two = jnp.sum(each * unit_sums[:, 0, :], axis=0)
    grad_shift_two = jnp.sum(grad_pooled, axis=0)

    core = (me & 1)[None]
    feed_parts = units // width
    feed = (gelu, slope, hidden_low, w_down, w_up, w_out)
    flying = []

    def begin(kept, sent, *more):
        one = Summing(kept, sent, *more)
        flying.append(one)
        return one

    def riding():
        for one in flying:
            if not one.left and not one.done:
                one.launch()
        return tuple(one.kept for one in flying)

    def landing(kept):
        for one, value in zip(list(flying), kept):
            one.kept = value
            one.left -= 1
            if not one.left:
                one.land()
            if one.done:
                flying.remove(one)

    chunks = [None]
    up_biases = []
    operands = (push, unit_two, inverse_two)
    for part in range(feed_parts):
        closing = part == feed_parts - 1
        second = part % 2
        if closing:
            operands = operands + (unit_one, inverse_one, mixed, row(gain_one))
        riders = riding()
        if part == 0:
            riders += tuple(act)
        tall_all = 2 * width + (width // 2 if part >= feed_parts - 2 else 0)
        grad_hidden, low, up_bias, rows, kept, sent, *landed = feed_back(
            lens, core, operands, *feed, part, feed_parts, second * width, tall_all,
            (kept, sent) if second else None, riders,
        )
        if part == 0:
            activations = Homing(landed, BF, seq_at, 1)
            activations.waiting.sort()
            flying.append(activations)
        else:
            landing(landed)
        up_biases.append(up_bias)
        if part == 0:
            rows_a, grad_low = rows, low
        operands = (grad_low, grad_hidden)
        if second:
            chunks.append(begin(kept, sent, None, (NEAR,), closing))
            if chunks[0] is None:
                chunks.pop(0)
    grad_one, grad_mixed, rows_b = grad_hidden, low, rows
    total, homes = None, ()
    bias = 0.0
    for first, count in ((0, mine - mine // 2), (mine - mine // 2, mine // 2)):
        closing = first > 0
        riders = riding()
        outs = attention_back(
            lens, src, core, n_seq, x, q, k, v, lse, grad_mixed, grad_one,
            (w_query, w_key, w_value), 0, 1, first, count, first, total, closing, homes, riders,
        )
        landing(outs[n_seq + (3 if closing else 2) :])
        homes, bias, total = outs[:n_seq], bias + outs[n_seq], outs[n_seq + 1]
    kept, sent = outs[n_seq + 1 : n_seq + 3]
    extra = jnp.concatenate(
        [
            bias, rows_b[0:3], rows_a[3:4], row(grad_gain_two), row(grad_shift_two),
            jnp.concatenate(up_biases, axis=1).reshape(feed_parts, width),
            jnp.zeros((-(8 + feed_parts) % 3, width), F32),
        ],
        axis=0,
    )
    heads = begin(kept, sent, extra.reshape(-1, 3 * width), (NEAR, FAR))
    homes = Homing(homes, F32, seq_at, 1)
    all_a, all_b = chunks
    attention = gathered = None
    every = lambda one: lax.all_gather(one.kept, BOTH, axis=0, tiled=True)
    gathered_a = every(all_a)
    steps = 0
    while flying or steps <= 2:
        if steps == 2:
            flying.append(homes)
        if all_b.done and gathered is None:
            gathered = every(all_b)
        if heads.done and attention is None:
            attention = Gathering(heads.kept)
            flying.append(attention)
        landing(tick(riding(), TICK if steps else BRIEF))
        steps += 1
    small = heads.extra.reshape(-1, width)
    attention = attention.kept
    all_a, all_b = in_order(gathered_a), in_order(gathered)
    activations, grad_tokens = activations.whole(), homes.whole()
    grads = [attention[:, n * width : (n + 1) * width].astype(F32) for n in range(3)]
    two = 2 * width
    half = two + width // 2
    again = half + width
    grad_down = jnp.concatenate([all_a[:two], all_b[:two]], axis=0).astype(F32)
    grad_out = jnp.concatenate(
        [all_b[two:half], all_b[again : again + width // 2]], axis=0
    ).astype(F32)
    grad_up = jnp.concatenate(
        [all_a[two : two + width], all_a[two + width :], all_b[half:again],
         all_b[again + width // 2 :]],
        axis=1,
    ).astype(F32)
    return (
        loss,
        activations,
        grad_tokens,
        grads[0],
        small[0],
        grads[1],
        grads[2],
        small[1],
        grad_out,
        small[4],
        small[2],
        small[3],
        grad_up,
        small[8 : 8 + feed_parts].reshape(units),
        grad_down,
        small[5],
        small[6],
        small[7],
    )


def solution(mesh):
    dp, seq = mesh.shape["dp"], mesh.shape["seq"]
    finer = jax.sharding.Mesh(mesh.devices.reshape(dp // 2, 2, seq // 2, 2), BOTH)
    in_specs = (P(DP, SEQ, None), P(), P(DP), P(), P(DP, None)) + (P(),) * 15
    out_specs = (P(), P(DP, SEQ, None), P(DP, SEQ, None)) + (P(),) * 15
    return jax.shard_map(local, mesh=finer, in_specs=in_specs, out_specs=out_specs, check_vma=False)
```

```python
import jax
import jax.numpy as jnp
from jax import lax
from jax.experimental import pallas as pl
from jax.experimental.pallas import tpu as pltpu
from jax.sharding import PartitionSpec as P

HEADS = 12
EPS = 1e-05
TEMPERATURE = 0.01
MASKED = -1000000000.0
SEQ = ("x", "core")
DP = ("far", "near")
BOTH = DP + SEQ
NEAR = ("near", "x")
FAR = ("far",)
EXACT = lax.Precision.HIGHEST
BF = jnp.bfloat16
F32 = jnp.float32
VMEM_BYTES = 60 * 2**20
BRIEF = pl.CostEstimate(flops=7 * 10**10, bytes_accessed=10**6, transcendentals=0)
LIGHT = pl.CostEstimate(flops=1000, bytes_accessed=1000, transcendentals=0)
TICK = pl.CostEstimate(flops=3 * 10**10, bytes_accessed=10**6, transcendentals=0)


def dot(left, right, left_at=1, right_at=0):
    return lax.dot_general(
        left, right, (((left_at,), (right_at,)), ((), ())), preferred_element_type=F32
    )


def normalize(value):
    centred = value - jnp.mean(value, axis=-1, keepdims=True)
    inverse = lax.rsqrt(jnp.mean(centred * centred, axis=-1, keepdims=True) + EPS)
    return centred * inverse, inverse


def norm_back(grad_unit, unit, inverse):
    first = jnp.mean(grad_unit, axis=-1, keepdims=True)
    second = jnp.mean(grad_unit * unit, axis=-1, keepdims=True)
    return inverse * (grad_unit - first - unit * second)


def gelu_and_slope(value):
    size = jnp.abs(value)
    t = 1.0 / (1.0 + (0.3275911 * 0.7071067811865476) * size)
    bell = jnp.exp(-0.5 * (value * value))
    tail = (
        (((0.5 * 1.061405429 * t - 0.5 * 1.453152027) * t + 0.5 * 1.421413741) * t
         - 0.5 * 0.284496736) * t + 0.5 * 0.254829592
    ) * t * bell
    below = jnp.where(value >= 0.0, 1.0 - tail, tail)
    return value * below, below + value * (bell * 0.3989422804014327)


def lane_half(width, which):
    lanes = lax.broadcasted_iota(jnp.int32, (1, width), 1)
    return ((lanes >= which * (width // 2)) & (lanes < (which + 1) * (width // 2))).astype(F32)


def whole(shape):
    return pl.BlockSpec(shape, lambda i, *_: (0,) * len(shape))


def per_passage(shape, first=0):
    return pl.BlockSpec((1,) + tuple(shape), lambda i, *_: (i + first,) + (0,) * len(shape))


ANYWHERE = pl.BlockSpec(memory_space=pl.ANY)


def fetch(sources, targets, sems):
    return [
        pltpu.make_async_copy(s, t, sems.at[i]) for i, (s, t) in enumerate(zip(sources, targets))
    ]


def forward_kernel(lens, src, *refs, pieces, first, aliased, riders):
    refs = list(refs)
    take = lambda n: [refs.pop(0) for _ in range(n)]
    x_in = take(pieces)
    hbm = take(6)
    (vectors,) = take(1)
    take(aliased + riders)
    (x_all, q_out, k_out, v_out, mixed_out, lse_out, unit_one_out, inverse_one_out,
     hidden_low_out, gelu_out, slope_out, unit_two_out, inverse_two_out, sums_out) = take(14)
    act = take(pieces)
    take(riders)
    held = take(6)
    act_held, sems = take(2)
    w_query, w_key, w_value, w_out, w_up, w_down = held
    b_query, b_value, b_out, gain_one, shift_one, b_down, gain_two, shift_two = (
        vectors[n : n + 1, :] for n in range(8)
    )
    step = pl.program_id(0)
    copies = fetch(hbm, held, sems)

    @pl.when(step == 0)
    def _():
        for copy in copies:
            copy.start()

    def ready(*which):
        @pl.when(step == 0)
        def _():
            for i in which:
                copies[i].wait()

    span, width = x_all.shape[1:]
    block = span // pieces
    head = width // HEADS
    pair = 2 * head
    length = lens[first + step]
    for k in range(pieces):
        x_all[0, pl.ds(pl.multiple_of(src[k] * block, block), block), :] = x_in[k][0]
    x = x_all[0]
    ready(0, 1, 2)
    q_out[0] = ((dot(x, w_query[...]) + b_query) * (head ** -0.5)).astype(BF)
    k_out[0] = dot(x, w_key[...]).astype(BF)
    v_out[0] = (dot(x, w_value[...]) + b_value).astype(BF)
    key_mask = jnp.where(
        lax.broadcasted_iota(jnp.int32, (1, span), 1) < length, 0.0, MASKED
    ).astype(F32)
    lanes = lax.broadcasted_iota(jnp.int32, (1, 128), 1)
    stats = jnp.zeros((span, 128), F32)
    for p in range(HEADS // 2):
        at = slice(p * pair, (p + 1) * pair)
        qp, kp, vp = q_out[0, :, at], k_out[0, :, at], v_out[0, :, at]
        total = None
        for h in range(2):
            half = lane_half(pair, h).astype(BF)
            scores = dot(qp, kp * half, 1, 1) + key_mask
            top = jnp.max(scores, axis=-1, keepdims=True)
            expo = jnp.exp(scores - top)
            norm = jnp.sum(expo, axis=-1, keepdims=True)
            low = (expo * (1.0 / norm)).astype(BF)
            term = dot(low, vp * half)
            total = term if total is None else total + term
            stats = jnp.where(lanes == 2 * p + h, top + jnp.log(norm), stats)
        mixed_out[0, :, at] = total.astype(BF)
    lse_out[0] = stats.T[: lse_out.shape[1]]
    ready(3)
    unit_one, inverse_one = normalize(x.astype(F32) + (dot(mixed_out[0], w_out[...]) + b_out))
    unit_one_out[0] = unit_one.astype(BF)
    inverse_one_out[0] = inverse_one
    hidden = unit_one * gain_one + shift_one
    hidden_low = hidden.astype(BF)
    hidden_low_out[0] = hidden_low
    ready(4, 5)
    total = hidden + b_down
    for c in range(gelu_out.shape[2] // width):
        at = slice(c * width, (c + 1) * width)
        value, slope = gelu_and_slope(dot(hidden_low, w_up[:, at]) + vectors[8 + c : 9 + c, :])
        low = value.astype(BF)
        gelu_out[0, :, at] = low
        slope_out[0, :, at] = slope.astype(BF)
        total = total + dot(low, w_down[at, :])
    unit_two, inverse_two = normalize(total)
    unit_two_out[0] = unit_two.astype(BF)
    inverse_two_out[0] = inverse_two
    act_held[...] = (unit_two * gain_two + shift_two).astype(BF)
    for k in range(pieces):
        act[k][0] = act_held[pl.ds(pl.multiple_of(src[k] * block, block), block), :]
    live = (lax.broadcasted_iota(jnp.int32, (span, 1), 0) < length).astype(F32)
    sums_out[0] = jnp.sum(unit_two * live, axis=0, keepdims=True)


def forward(lens, src, pieces, weights, vectors, passages, first, before, riders):
    count, block, width = pieces[0].shape
    n = len(pieces)
    span = block * n
    units = weights[4].shape[1]
    shapes = [
        ((span, width), BF), ((span, width), BF), ((span, width), BF), ((span, width), BF),
        ((span, width), BF), ((16, span), F32), ((span, width), BF), ((span, 1), F32),
        ((span, width), BF), ((span, units), BF), ((span, units), BF), ((span, width), BF),
        ((span, 1), F32), ((1, width), F32),
    ]
    outs = [jax.ShapeDtypeStruct((passages,) + s, t) for s, t in shapes]
    outs += [jax.ShapeDtypeStruct((passages, block, width), BF)] * n
    out_specs = [per_passage(o.shape[1:], first) for o in outs]
    kinds = len(outs)
    in_specs = [per_passage((block, width))] * n + [ANYWHERE] * 6 + [whole(vectors.shape)]
    operands = list(pieces) + list(weights) + [vectors]
    aliases = {}
    if before is not None:
        for i, value in enumerate(before):
            aliases[2 + len(operands)] = i
            operands.append(value)
            in_specs.append(ANYWHERE)
    aliases.update(alias(operands, in_specs, outs, out_specs, riders, 2))

    def kernel(*refs):
        forward_kernel(
            *refs, pieces=n, first=first, aliased=0 if before is None else kinds,
            riders=len(riders),
        )

    return pl.pallas_call(
        kernel,
        out_shape=outs,
        grid_spec=pltpu.PrefetchScalarGridSpec(
            num_scalar_prefetch=2,
            grid=(count,),
            in_specs=in_specs,
            out_specs=out_specs,
            scratch_shapes=[pltpu.VMEM(w.shape, BF) for w in weights]
            + [pltpu.VMEM((span, width), BF), pltpu.SemaphoreType.DMA((6,))],
        ),
        input_output_aliases=aliases,
        compiler_params=pltpu.CompilerParams(vmem_limit_bytes=VMEM_BYTES),
        cost_estimate=BRIEF,
    )(lens, src, *operands)


def second_norm_back(length, push, unit_two, inverse_two):
    live = lax.broadcasted_iota(jnp.int32, (unit_two.shape[0], 1), 0) < length
    return jnp.where(live, norm_back(push, unit_two, inverse_two), 0.0)


def hand_over(total, kept_hbm, sent_hbm, side, row, column, sems):
    half, columns = total.shape[0] // 2, total.shape[1]
    own = pl.multiple_of(side * half, half)
    other = pl.multiple_of((1 - side) * half, half)
    copies = [
        pltpu.make_async_copy(
            total.at[pl.ds(at, half), :],
            out.at[pl.ds(row, half), pl.ds(column, columns)],
            sem,
        )
        for at, out, sem in ((own, kept_hbm, sems.at[0]), (other, sent_hbm, sems.at[1]))
    ]
    for copy in copies:
        copy.start()
    for copy in copies:
        copy.wait()


def alias(operands, specs, outs, out_specs, values, offset):
    pairs = {}
    for value in values:
        pairs[offset + len(operands)] = len(outs)
        operands.append(value)
        specs.append(ANYWHERE)
        outs.append(jax.ShapeDtypeStruct(value.shape, value.dtype))
        out_specs.append(ANYWHERE)
    return pairs


def feed_kernel(lens, core, *refs, part, parts, place, filling, riders):
    refs = list(refs)
    take = lambda n: [refs.pop(0) for _ in range(n)]
    opening, closing = part == 0, part == parts - 1
    if opening:
        push, unit_two, inverse_two = take(3)
    else:
        grad_low_in, grad_hidden_in = take(2)
    if closing:
        unit_one, inverse_one, mixed, gain_one = take(4)
    gelu, slope, hidden_low, w_down, w_up = take(5)
    if closing:
        (w_out,) = take(1)
    take((2 if filling else 0) + riders)
    grad_hidden_out, low_out, up_bias, rows = take(4)
    kept_hbm, sent_hbm = take(2)
    take(riders)
    total, sems = take(2)
    step = pl.program_id(0)
    last = pl.num_programs(0) - 1
    units, width = w_down.shape

    @pl.when(step == 0)
    def _():
        total[...] = jnp.zeros_like(total)
        up_bias[...] = jnp.zeros_like(up_bias)
        rows[...] = jnp.zeros_like(rows)

    if opening:
        grad_hidden = second_norm_back(
            lens[step], push[0], unit_two[0].astype(F32), inverse_two[0]
        )
        grad_low = grad_hidden.astype(BF)
        low_out[0] = grad_low
        rows[3:4, :] += jnp.sum(grad_low.astype(F32), axis=0, keepdims=True)
    else:
        grad_hidden = grad_hidden_in[0]
        grad_low = grad_low_in[0]
    up_low = (dot(grad_low, w_down[...], 1, 1) * slope[0].astype(F32)).astype(BF)
    total[:units, :] += dot(gelu[0], grad_low, 0, 0)
    up_bias[...] += jnp.sum(up_low.astype(F32), axis=0, keepdims=True)
    total[total.shape[0] - width :, :] += dot(hidden_low[0], up_low, 0, 0)
    grad_hidden = grad_hidden + dot(up_low, w_up[...], 1, 1)
    if closing:
        unit = unit_one[0].astype(F32)
        rows[0:1, :] += jnp.sum(grad_hidden * unit, axis=0, keepdims=True)
        rows[1:2, :] += jnp.sum(grad_hidden, axis=0, keepdims=True)
        grad_one = norm_back(grad_hidden * gain_one[...], unit, inverse_one[0])
        grad_hidden_out[0] = grad_one
        branch_low = grad_one.astype(BF)
        rows[2:3, :] += jnp.sum(branch_low.astype(F32), axis=0, keepdims=True)
        total[units : units + width, :] += dot(mixed[0], branch_low, 0, 0)
        low_out[0] = dot(branch_low, w_out[...], 1, 1).astype(BF)
    else:
        grad_hidden_out[0] = grad_hidden

    @pl.when(step == last)
    def _():
        hand_over(total, kept_hbm, sent_hbm, core[0], place, 0, sems)


def feed_back(lens, core, row_operands, gelu, slope, hidden_low, w_down, w_up, w_out, part, parts,
              place, tall_all, filled, riders):
    opening, closing = part == 0, part == parts - 1
    passages, span, units = gelu.shape
    units //= parts
    width = w_down.shape[1]
    tall = 2 * units + (width if closing else 0)
    tile = per_passage((span, width))
    column = per_passage((span, 1))
    chunk = pl.BlockSpec((1, span, units), lambda i, *_: (i, 0, part))
    specs = [per_passage((1, width)), tile, column] if opening else [tile, tile]
    operands = list(row_operands)
    if closing:
        specs += [tile, column, tile, whole((1, width))]
    operands += [gelu, slope, hidden_low, w_down, w_up]
    specs += [
        chunk, chunk, tile,
        pl.BlockSpec((units, width), lambda i, *_: (part, 0)),
        pl.BlockSpec((width, units), lambda i, *_: (0, part)),
    ]
    if closing:
        operands.append(w_out)
        specs.append(whole((width, width)))
    like = lambda t: jax.ShapeDtypeStruct((passages, span, width), t)
    outs = [
        like(F32), like(BF), jax.ShapeDtypeStruct((1, units), F32),
        jax.ShapeDtypeStruct((8, width), F32),
    ]
    out_specs = [tile, tile, whole((1, units)), whole((8, width))]
    if filled is None:
        outs += [jax.ShapeDtypeStruct((tall_all, width), F32)] * 2
        out_specs += [ANYWHERE] * 2
        pairs = alias(operands, specs, outs, out_specs, riders, 2)
    else:
        pairs = alias(operands, specs, outs, out_specs, tuple(filled) + tuple(riders), 2)

    def kernel(*refs):
        feed_kernel(
            *refs, part=part, parts=parts, place=place, filling=filled is not None,
            riders=len(riders),
        )

    return pl.pallas_call(
        kernel,
        out_shape=outs,
        grid_spec=pltpu.PrefetchScalarGridSpec(
            num_scalar_prefetch=2,
            grid=(passages,),
            in_specs=specs,
            out_specs=out_specs,
            scratch_shapes=[pltpu.VMEM((tall, width), F32), pltpu.SemaphoreType.DMA((2,))],
        ),
        input_output_aliases=pairs,
        compiler_params=pltpu.CompilerParams(vmem_limit_bytes=VMEM_BYTES),
        cost_estimate=BRIEF,
    )(lens, core, *operands)


def attention_kernel(
    lens, src, core, *refs, pieces, final, part, first, opening, closing, filled, riders
):
    refs = list(refs)
    take = lambda n: [refs.pop(0) for _ in range(n)]
    x, q, k, v, lse, grad_mixed, grad_in = take(7)
    weights = take(3)
    if not opening:
        (total_in,) = take(1)
    take(filled + riders)
    out = take(pieces if final else 1)
    (bias,) = take(1)
    totals_out = take(2 if closing else 1)
    take(riders)
    total = take(1)[0]
    lows = take(3)
    tokens_low, sems = take(2)
    step = pl.program_id(0)
    last = pl.num_programs(0) - 1
    span, columns = q.shape[1:]
    width = x.shape[2]
    block = span // pieces
    head = width // HEADS
    pair = 2 * head
    scale = head ** -0.5
    if not opening:
        before = pltpu.make_async_copy(total_in, total, sems.at[0])

    @pl.when(step == 0)
    def _():
        if opening:
            total[...] = jnp.zeros_like(total)
        else:
            before.start()
        bias[...] = jnp.zeros_like(bias)

    key_mask = jnp.where(
        lax.broadcasted_iota(jnp.int32, (span, 1), 0) < lens[first + step], 0.0, MASKED
    ).astype(F32)
    query_low, key_low, value_low = lows
    for p in range(columns // pair):
        at = slice(p * pair, (p + 1) * pair)
        qp, kp, vp, gp = q[0, :, at], k[0, :, at], v[0, :, at], grad_mixed[0, :, at]
        gq = gk = gv = None
        for h in range(2):
            half = lane_half(pair, h).astype(BF)
            qm, gm, km = qp * half, gp * half, kp * half
            n = part * (columns // head) + 2 * p + h
            probs = jnp.exp((dot(kp, qm, 1, 1) + key_mask) - lse[0, n : n + 1, :])
            low = probs.astype(BF)
            grad_probs = dot(vp, gm, 1, 1)
            delta = jnp.sum(probs * grad_probs, axis=0, keepdims=True)
            scores = (probs * (grad_probs - delta)).astype(BF)
            tv = dot(low, gm)
            tk = dot(scores, qm)
            tq = dot(scores, km, 0, 0)
            gv = tv if gv is None else gv + tv
            gk = tk if gk is None else gk + tk
            gq = tq if gq is None else gq + tq
        query_low[:, at] = (gq * scale).astype(BF)
        key_low[:, at] = gk.astype(BF)
        value_low[:, at] = gv.astype(BF)

    if not opening:

        @pl.when(step == 0)
        def _():
            before.wait()

    grad = grad_in[0]
    for n, (low, weight) in enumerate(zip(lows, weights)):
        grad = grad + dot(low[...], weight[...], 1, 1)
        total[:, n * columns : (n + 1) * columns] += dot(x[0], low[...], 0, 0)
    bias[0:1, :] += jnp.sum(query_low[...].astype(F32), axis=0, keepdims=True)
    bias[1:2, :] += jnp.sum(value_low[...].astype(F32), axis=0, keepdims=True)
    if final:
        tokens_low[...] = grad.astype(BF)
        for n in range(pieces):
            out[n][0] = tokens_low[pl.ds(pl.multiple_of(src[n] * block, block), block), :]
    else:
        out[0][0] = grad

    @pl.when(step == last)
    def _():
        if closing:
            hand_over(total, *totals_out, core[0], 0, 0, sems)
        else:
            after = pltpu.make_async_copy(total, totals_out[0], sems.at[1])
            after.start()
            after.wait()


def attention_back(lens, src, core, pieces, x, q, k, v, lse, grad_mixed, grad_in, weights, part,
                   parts, first, count, grad_first, total, closing, before, riders):
    passages, span, width = x.shape
    block = span // pieces
    columns = width // parts
    final = part == parts - 1
    tall = width

    def kernel(*refs):
        attention_kernel(
            *refs, pieces=pieces, final=final, part=part, first=first, opening=total is None,
            closing=closing, filled=len(before), riders=len(riders),
        )

    tile = per_passage((span, width), first)
    chunk = pl.BlockSpec((1, span, columns), lambda i, *_: (i + first, 0, part))
    if final:
        outs = [jax.ShapeDtypeStruct((passages, block, width), BF)] * pieces
        out_specs = [per_passage((block, width), first)] * pieces
    else:
        outs = [jax.ShapeDtypeStruct((count, span, width), F32)]
        out_specs = [per_passage((span, width))]
    outs.append(jax.ShapeDtypeStruct((2, columns), F32))
    out_specs.append(whole((2, columns)))
    if closing:
        outs += [jax.ShapeDtypeStruct((tall // 2, 3 * columns), F32)] * 2
        out_specs += [ANYWHERE] * 2
    else:
        outs.append(jax.ShapeDtypeStruct((tall, 3 * columns), F32))
        out_specs.append(ANYWHERE)
    operands = [x, q, k, v, lse, grad_mixed, grad_in, *weights]
    specs = [tile, chunk, chunk, chunk, per_passage(lse.shape[1:], first), chunk]
    specs.append(per_passage((span, width), grad_first))
    specs += [pl.BlockSpec((width, columns), lambda i, *_: (0, part))] * 3
    if total is not None:
        operands.append(total)
        specs.append(ANYWHERE)
    pairs = {}
    for i, value in enumerate(before):
        pairs[3 + len(operands)] = i
        operands.append(value)
        specs.append(ANYWHERE)
    pairs.update(alias(operands, specs, outs, out_specs, riders, 3))
    return pl.pallas_call(
        kernel,
        out_shape=outs,
        grid_spec=pltpu.PrefetchScalarGridSpec(
            num_scalar_prefetch=3,
            grid=(count,),
            in_specs=specs,
            out_specs=out_specs,
            scratch_shapes=[pltpu.VMEM((tall, 3 * columns), F32)]
            + [pltpu.VMEM((span, columns), BF)] * 3
            + [pltpu.VMEM((span, width), BF), pltpu.SemaphoreType.DMA((2,))],
        ),
        input_output_aliases=pairs,
        compiler_params=pltpu.CompilerParams(vmem_limit_bytes=VMEM_BYTES),
        cost_estimate=BRIEF,
    )(lens, src, core, *operands)


def tick(values, cost):
    operands, specs, outs, out_specs = [], [], [], []
    pairs = alias(operands, specs, outs, out_specs, values, 0)
    return pl.pallas_call(
        lambda *refs: None,
        out_shape=outs,
        in_specs=specs,
        out_specs=out_specs,
        input_output_aliases=pairs,
        cost_estimate=cost,
    )(*operands)


def flip(value, amount, axes, devices):
    return lax.ppermute(value, axes, [(i, i ^ amount) for i in range(devices)])


def land_kernel(at, kept, came, low, own):
    value = kept[...] + came[...]
    low[...] = value.astype(BF)

    @pl.when(pl.program_id(0) == at[0])
    def _():
        own[...] = value


def land_first(kept, came, at, n):
    rows, width = kept.shape
    part = rows // n
    each = pl.BlockSpec((part, width), lambda i, *_: (i, 0))
    return pl.pallas_call(
        land_kernel,
        out_shape=[
            jax.ShapeDtypeStruct((rows, width), BF), jax.ShapeDtypeStruct((part, width), F32)
        ],
        grid_spec=pltpu.PrefetchScalarGridSpec(
            num_scalar_prefetch=1,
            grid=(n,),
            in_specs=[each, each],
            out_specs=[each, whole((part, width))],
        ),
        compiler_params=pltpu.CompilerParams(vmem_limit_bytes=VMEM_BYTES),
        cost_estimate=LIGHT,
    )(at[None], kept, came)


def exchange(blocks, axes):
    return lax.all_to_all(blocks, axes, split_axis=0, concat_axis=0, tiled=True)


class Summing:
    def __init__(self, kept, sent, extra=None, narrow=(NEAR,), hops=False):
        self.kept, self.sent, self.extra = kept, sent, extra
        self.narrow, self.hops = narrow, hops
        self.stages = [None, NEAR, FAR]
        self.left = 0
        self.done = False
        self.apart = None

    def launch(self):
        self.axes = self.stages.pop(0)
        self.left = 1
        if self.axes is None:
            self.came = flip(self.sent, 1, BOTH, lax.axis_size(BOTH))
            if self.extra is not None:
                self.apart = flip(self.extra, 1, BOTH, lax.axis_size(BOTH))
            return
        n = lax.axis_size(self.axes)
        rows, width = self.kept.shape
        sent = self.value.reshape(n, rows, width)
        if self.axes is FAR and self.hops:
            at = lax.axis_index(FAR)
            self.came = [
                flip(lax.dynamic_index_in_dim(sent, at ^ k, 0, False), k, FAR, n)
                for k in range(1, n)
            ]
            self.left = 2
            return
        spread = lambda v: jnp.broadcast_to(v[None], (n,) + v.shape)
        more = []
        if self.axes in self.narrow:
            sent = sent.astype(BF)
            if self.extra is not None:
                high = lax.reduce_precision(self.extra, 8, 7)
                low = lax.reduce_precision(self.extra - high, 8, 7)
                self.extra = high + low
                more = [spread(high.astype(BF)), spread(low.astype(BF))]
        elif self.extra is not None:
            more = [spread(self.extra)]
        self.came = exchange(jnp.concatenate([sent] + more, axis=1) if more else sent, self.axes)

    def land(self):
        rows = self.kept.shape[0]
        if isinstance(self.came, list):
            self.kept = sum(self.came, self.kept).astype(BF)
            self.left, self.done = 0, True
            return
        came = self.came.astype(F32)
        if self.axes is None:
            if self.extra is not None:
                self.extra = self.extra + self.apart
            self.value, self.kept = land_first(
                self.kept, came, lax.axis_index(NEAR), lax.axis_size(NEAR)
            )
            self.left = 0
            return
        else:
            other = jnp.arange(came.shape[0]) != lax.axis_index(self.axes)
            value = self.kept + jnp.sum(
                jnp.where(other[:, None, None], came[:, :rows], 0.0), axis=0
            )
            if self.extra is not None:
                more = jnp.sum(came[:, rows:], axis=0)
                self.extra = jnp.sum(more.reshape((-1,) + self.extra.shape), axis=0)
        self.left = 0
        if not self.stages:
            self.kept = value.astype(BF)
            self.done = True
            return
        self.value = value
        part = value.shape[0] // lax.axis_size(self.stages[0])
        self.kept = lax.dynamic_slice_in_dim(
            value, lax.axis_index(self.stages[0]) * part, part
        )


class Gathering:
    def __init__(self, value):
        self.kept = value
        self.stages = [FAR, NEAR, None]
        self.left = 0
        self.done = False

    def launch(self):
        self.axes = self.stages.pop(0)
        self.left = 1
        if self.axes is None:
            self.came = flip(self.kept, 1, BOTH, lax.axis_size(BOTH))
        else:
            n = lax.axis_size(self.axes)
            self.came = exchange(
                jnp.broadcast_to(self.kept[None], (n,) + self.kept.shape), self.axes
            )

    def land(self):
        if self.axes is None:
            self.kept = jnp.where(
                lax.axis_index("core") == 0,
                jnp.concatenate([self.kept, self.came], axis=0),
                jnp.concatenate([self.came, self.kept], axis=0),
            )
        else:
            own = jnp.arange(self.came.shape[0]) == lax.axis_index(self.axes)
            self.kept = jnp.where(own[:, None, None], self.kept[None], self.came).reshape(
                -1, self.kept.shape[1]
            )
        self.left = 0
        self.done = not self.stages


class Homing:
    def __init__(self, pieces, kind, seq_at, stretch):
        n = len(pieces)
        mine, block, width = pieces[0].shape
        self.kind, self.seq_at, self.stretch = kind, seq_at, stretch
        self.kept = jnp.zeros((n, mine, block, width), kind)
        self.waiting = [(k, pieces[k]) for k in (*range(2, n), 1)[: n - 1]]
        self.place(0, pieces[0])
        self.came = []
        self.left = 0
        self.done = False
        self.n = n

    def place(self, k, piece):
        self.kept = lax.dynamic_update_slice_in_dim(
            self.kept, piece.astype(self.kind)[None], self.seq_at ^ k, 0
        )

    def launch(self):
        take = max(1, (self.n - 1) // 3)
        self.came = [(k, flip(p, k, SEQ, self.n)) for k, p in self.waiting[:take]]
        self.waiting = self.waiting[take:]
        self.left = self.stretch

    def land(self):
        for k, piece in self.came:
            self.place(k, piece)
        self.left = 0
        self.done = not self.waiting

    def whole(self):
        n, mine, block, width = self.kept.shape
        return self.kept.reshape(n * mine, block, width)


def in_order(every):
    n_far, n_near, n_x, n_core = (lax.axis_size(axis) for axis in BOTH)
    width = every.shape[1]
    every = every.reshape(n_far, n_near, n_x, n_core, -1, width)
    return every.transpose(3, 1, 2, 0, 4, 5).reshape(-1, width)


def local(
    tokens, sources, lengths, pairing, queries, w_query, b_query, w_key, w_value, b_value, w_out,
    b_out, gain_one, shift_one, w_up, b_up, w_down, second_feedforward_offset, gain_two, shift_two,
):
    documents, block, width = tokens.shape
    n_seq, n_dp = lax.axis_size(SEQ), lax.axis_size(DP)
    devices = n_seq * n_dp
    seq_at, dp_at = lax.axis_index(SEQ), lax.axis_index(DP)
    me = dp_at * n_seq + seq_at
    mine = documents // n_seq
    batch = documents * n_dp
    units = w_up.shape[1]
    src = seq_at ^ jnp.arange(n_seq, dtype=jnp.int32)
    lens = lax.dynamic_slice_in_dim(lengths, seq_at * mine, mine)

    def arriving(first, count, before):
        late = 0
        if before is not None:
            late = (before[0, 0, 0] != before[0, 0, 0]).astype(jnp.int32)
        pieces = []
        for k in range(n_seq):
            rows = lax.dynamic_slice_in_dim(tokens, (seq_at ^ k) * mine + first + late, count)
            pieces.append(rows if k == 0 else flip(rows, k, SEQ, n_seq))
        return pieces, rows

    weights = (w_query, w_key, w_value, w_out, w_up, w_down)
    row = lambda v: v[None, :]
    vectors = [b_query, b_value, b_out, gain_one, shift_one, second_feedforward_offset, gain_two,
               shift_two, b_up]
    vectors = jnp.concatenate(vectors).reshape(-1, width)
    saved = None
    first = 0
    sent = None
    dp_hops = n_dp.bit_length() - 1
    hop = lambda value, bit: flip(value, 1 << bit, DP, n_dp)
    spread = queries[None]
    done = min(1, dp_hops)
    if done:
        spread = jnp.concatenate([spread, hop(spread, 0)], axis=0)
    for count in (1, mine - 1):
        pieces, sent = arriving(first, count, sent)
        came = [hop(spread, done)] if done < dp_hops else []
        *saved, spread = forward(
            lens, src, pieces, weights, vectors, mine, first, saved, (spread,)
        )
        spread = jnp.concatenate([spread] + came, axis=0)
        done += len(came)
        first += count
    for bit in range(done, dp_hops):
        spread = jnp.concatenate([spread, hop(spread, bit)], axis=0)
    (x, q, k, v, mixed, lse, unit_one, inverse_one, hidden_low, gelu, slope, unit_two, inverse_two,
     unit_sums) = saved[:14]
    act = saved[14:]

    asked = jnp.concatenate(
        [lax.dynamic_index_in_dim(spread, dp_at ^ i, 0, False) for i in range(n_dp)], axis=0
    ).astype(F32)
    asked = asked * lax.rsqrt(jnp.sum(asked * asked, axis=-1, keepdims=True) + 1e-06)
    count = lens.astype(F32)[:, None]
    pooled = (unit_sums[:, 0, :] * gain_two + count * shift_two) / count
    pooled_inverse = lax.rsqrt(jnp.sum(pooled * pooled, axis=-1, keepdims=True) + 1e-06)
    pooled_unit = pooled * pooled_inverse
    own = jnp.dot(pooled_unit, asked.T, precision=EXACT) / TEMPERATURE
    scores = own[None]
    for bit in range(devices.bit_length() - 1):
        scores = jnp.concatenate([scores, flip(scores, 1 << bit, BOTH, devices)], axis=0)
    scores = scores.reshape(batch, batch)
    everyone = jnp.arange(batch, dtype=jnp.int32)
    order = ((me ^ jnp.arange(devices, dtype=jnp.int32))[:, None] * mine
             + jnp.arange(mine, dtype=jnp.int32)[None, :]).reshape(batch)
    pick = lambda index: jnp.sum(
        jnp.where(index[:, None] == everyone[None, :], sources[None, :], 0), axis=1
    )
    same = pick(order)[:, None] == pick(pairing)[None, :]
    match = order[:, None] == pairing[None, :]
    scores = jnp.where(same, scores, MASKED)
    top = jnp.max(scores, axis=0)
    log_total = top + jnp.log(jnp.sum(jnp.exp(scores - top), axis=0))
    chosen = jnp.sum(jnp.where(match, scores, 0.0), axis=0)
    loss = jnp.sum(log_total - chosen) / batch
    grad_scores = (jnp.exp(scores[:mine] - log_total) - match[:mine].astype(F32)) * (
        1.0 / batch / TEMPERATURE
    )
    grad_unit = jnp.dot(grad_scores, asked, precision=EXACT)
    grad_pooled = pooled_inverse * (
        grad_unit - pooled_unit * jnp.sum(grad_unit * pooled_unit, axis=-1, keepdims=True)
    )
    each = grad_pooled / count
    push = (each * gain_two)[:, None, :]
    grad_gain_two = jnp.sum(each * unit_sums[:, 0, :], axis=0)
    grad_shift_two = jnp.sum(grad_pooled, axis=0)

    core = (me & 1)[None]
    feed_parts = units // width
    feed = (gelu, slope, hidden_low, w_down, w_up, w_out)
    flying = []

    def begin(kept, sent, *more):
        one = Summing(kept, sent, *more)
        flying.append(one)
        return one

    def riding():
        for one in flying:
            if not one.left and not one.done:
                one.launch()
        return tuple(one.kept for one in flying)

    def landing(kept):
        for one, value in zip(list(flying), kept):
            one.kept = value
            one.left -= 1
            if not one.left:
                one.land()
            if one.done:
                flying.remove(one)

    chunks = [None]
    up_biases = []
    operands = (push, unit_two, inverse_two)
    for part in range(feed_parts):
        closing = part == feed_parts - 1
        second = part % 2
        if closing:
            operands = operands + (unit_one, inverse_one, mixed, row(gain_one))
        riders = riding()
        if part == 0:
            riders += tuple(act)
        tall_all = 2 * width + (width // 2 if part >= feed_parts - 2 else 0)
        grad_hidden, low, up_bias, rows, kept, sent, *landed = feed_back(
            lens, core, operands, *feed, part, feed_parts, second * width, tall_all,
            (kept, sent) if second else None, riders,
        )
        if part == 0:
            activations = Homing(landed, BF, seq_at, 1)
            activations.waiting.sort()
            flying.append(activations)
        else:
            landing(landed)
        up_biases.append(up_bias)
        if part == 0:
            rows_a, grad_low = rows, low
        operands = (grad_low, grad_hidden)
        if second:
            chunks.append(begin(kept, sent, None, (NEAR,), closing))
            if chunks[0] is None:
                chunks.pop(0)
    grad_one, grad_mixed, rows_b = grad_hidden, low, rows
    total, homes = None, ()
    bias = 0.0
    for first, count in ((0, mine - mine // 2), (mine - mine // 2, mine // 2)):
        closing = first > 0
        riders = riding()
        outs = attention_back(
            lens, src, core, n_seq, x, q, k, v, lse, grad_mixed, grad_one,
            (w_query, w_key, w_value), 0, 1, first, count, first, total, closing, homes, riders,
        )
        landing(outs[n_seq + (3 if closing else 2) :])
        homes, bias, total = outs[:n_seq], bias + outs[n_seq], outs[n_seq + 1]
    kept, sent = outs[n_seq + 1 : n_seq + 3]
    extra = jnp.concatenate(
        [
            bias, rows_b[0:3], rows_a[3:4], row(grad_gain_two), row(grad_shift_two),
            jnp.concatenate(up_biases, axis=1).reshape(feed_parts, width),
            jnp.zeros((-(8 + feed_parts) % 3, width), F32),
        ],
        axis=0,
    )
    heads = begin(kept, sent, extra.reshape(-1, 3 * width), (NEAR, FAR))
    homes = Homing(homes, F32, seq_at, 1)
    all_a, all_b = chunks
    attention = gathered = None
    every = lambda one: lax.all_gather(one.kept, BOTH, axis=0, tiled=True)
    gathered_a = every(all_a)
    steps = 0
    while flying or steps <= 2:
        if steps == 2:
            flying.append(homes)
        if all_b.done and gathered is None:
            gathered = every(all_b)
        if heads.done and attention is None:
            attention = Gathering(heads.kept)
            flying.append(attention)
        landing(tick(riding(), TICK if steps else BRIEF))
        steps += 1
    small = heads.extra.reshape(-1, width)
    attention = attention.kept
    all_a, all_b = in_order(gathered_a), in_order(gathered)
    activations, grad_tokens = activations.whole(), homes.whole()
    grads = [attention[:, n * width : (n + 1) * width].astype(F32) for n in range(3)]
    two = 2 * width
    half = two + width // 2
    again = half + width
    grad_down = jnp.concatenate([all_a[:two], all_b[:two]], axis=0).astype(F32)
    grad_out = jnp.concatenate(
        [all_b[two:half], all_b[again : again + width // 2]], axis=0
    ).astype(F32)
    grad_up = jnp.concatenate(
        [all_a[two : two + width], all_a[two + width :], all_b[half:again],
         all_b[again + width // 2 :]],
        axis=1,
    ).astype(F32)
    return (
        loss,
        activations,
        grad_tokens,
        grads[0],
        small[0],
        grads[1],
        grads[2],
        small[1],
        grad_out,
        small[4],
        small[2],
        small[3],
        grad_up,
        small[8 : 8 + feed_parts].reshape(units),
        grad_down,
        small[5],
        small[6],
        small[7],
    )


def solution(mesh):
    dp, seq = mesh.shape["dp"], mesh.shape["seq"]
    finer = jax.sharding.Mesh(mesh.devices.reshape(dp // 2, 2, seq // 2, 2), BOTH)
    in_specs = (P(DP, SEQ, None), P(), P(DP), P(), P(DP, None)) + (P(),) * 15
    out_specs = (P(), P(DP, SEQ, None), P(DP, SEQ, None)) + (P(),) * 15
    return jax.shard_map(local, mesh=finer, in_specs=in_specs, out_specs=out_specs, check_vma=False)
```
